512 devices in a mesh: gx: 32 (over y, x_lo, core), gy: 16 (over z, x_hi).
Axes of the slice: x: 4 (x_hi: 2, x_lo: 2; x = x_hi * 2 + x_lo), y: 8, z: 8, core: 2. Of those that a mesh axis runs over, the one named last changes fastest.
Arguments:
- noisy: float32 [256, 128, 128], P('gx', 'gy'), may hold values from -6 to 6
- weights: float32 [2, 256, 128, 128], P(None, 'gx', 'gy'), may hold values from 0.1 to 1
- filter_in: bfloat16 [2, 64, 27], replicated, may hold values from -1.25 to 1.25
- bias: float32 [2, 64], replicated, may hold values from -3 to 3
- filter_out: bfloat16 [2, 27, 64], replicated, may hold values from -0.75 to 0.75
- upstream: float32 [256, 128, 128], P('gx', 'gy'), may hold values from -6 to 6
Outputs:
- grad_input: float32 [256, 128, 128], P('gx', 'gy')
- grad_w1: float32 [2, 64, 27], replicated
- grad_w2: float32 [2, 27, 64], replicated
- grad_bias: float32 [2, 64], replicated
The draws below stay inside these ranges and needn't reach their ends.
All inputs are finite; a program needn't handle non-finite values.
Results may differ from the reference program's by a relative error of at most 0.0062.
Values may be sent and summed in bfloat16 or wider, within the bound.
A program may use at most 64 MiB of HBM per device.

```python
import math
import jax
import jax.numpy as jnp
from jax import lax

CH = 64
LAYERS = 2
NZ = 128
NX = 256
NY = 128


def levels(own_key, dims, split, low, high):
    def one(axis_at, blocks):
        draws = jax.random.uniform(jax.random.fold_in(jax.random.fold_in(own_key, 6), axis_at), (blocks,), jnp.float32, low / len(split), high / len(split))
        return jnp.repeat(jnp.exp(draws), dims[axis_at] // blocks).reshape((-1,) + (1,) * (len(dims) - axis_at - 1))

    factor_of = one(*split[0])
    for cut in split[1:]:
        factor_of = factor_of * one(*cut)
    return factor_of


def bell_draw(stream_key, extent, deviation, limit, split=(), kind=jnp.bfloat16):
    result = jax.random.normal(stream_key, extent, jnp.float32) * deviation
    if len(split) > 0:
        result = levels(stream_key, extent, split, -0.22, 0.18) * result
    return jnp.clip(result, min=-limit, max=limit).astype(kind)


def setup_inputs(seed: int = 0) -> dict:
    keys = jax.random.split(jax.random.key(seed), 7)
    return {
        "noisy": bell_draw(keys[0], (NX, NY, NZ), 1.0, 6.0, ((0, 32), (1, 16)), jnp.float32),
        "weights": jnp.clip(jnp.exp(math.log(1.0) - 2.3025851 * jax.random.uniform(keys[1], (LAYERS, NX, NY, NZ), jnp.float32) ** levels(keys[1], (LAYERS, NX, NY, NZ), ((1, 32), (2, 16)), -0.2, 0.2)), 0.1, 1.0),
        "filter_in": bell_draw(keys[2], (LAYERS, CH, 27), 27 ** -0.5, 1.25),
        "bias": bell_draw(keys[3], (LAYERS, CH), 0.5, 3.0, (), jnp.float32),
        "filter_out": bell_draw(keys[4], (LAYERS, 27, CH), CH ** -0.5, 0.75),
        "upstream": bell_draw(keys[5], (NX, NY, NZ), 1.0, 6.0, ((0, 32), (1, 16)), jnp.float32),
    }


TAU = 0.15
LAMB = 1.0

def padding_depth_extent(field):
    widths = [(0, 0)] * (field.ndim - 1) + [(1, 1)]
    return jnp.pad(field, widths)

def stack_offsets(padded, sign):
    n0 = padded.shape[-3] - 2
    n1 = padded.shape[-2] - 2
    n2 = padded.shape[-1] - 2
    parts = []
    for dx in (-1, 0, 1):
        for dy in (-1, 0, 1):
            for dz in (-1, 0, 1):
                a0 = 1 + sign * dx
                a1 = 1 + sign * dy
                a2 = 1 + sign * dz
                parts.append(padded[..., a0:a0 + n0, a1:a1 + n1, a2:a2 + n2])
    return jnp.stack(parts, axis=-4)

def spread_total_sum(padded, sign):
    n0 = padded.shape[-3] - 2
    n1 = padded.shape[-2] - 2
    n2 = padded.shape[-1] - 2
    total = padded[0, 1 - sign:1 - sign + n0, 1 - sign:1 - sign + n1, 1 - sign:1 - sign + n2]
    index = 0
    for dx in (-1, 0, 1):
        for dy in (-1, 0, 1):
            for dz in (-1, 0, 1):
                if index > 0:
                    a0 = 1 + sign * dx
                    a1 = 1 + sign * dy
                    a2 = 1 + sign * dz
                    total = total + padded[index, a0:a0 + n0, a1:a1 + n1, a2:a2 + n2]
                index += 1
    return total

def stencil_kernel(value_padded, weight_padded):
    value_vertical = padding_depth_extent(value_padded)
    wz = padding_depth_extent(weight_padded)
    flux_x = wz[:-1, 1:-1, 1:-1] * (value_vertical[1:, 1:-1, 1:-1] - value_vertical[:-1, 1:-1, 1:-1])
    flux_y = wz[1:-1, :-1, 1:-1] * (value_vertical[1:-1, 1:, 1:-1] - value_vertical[1:-1, :-1, 1:-1])
    flux_z = wz[1:-1, 1:-1, :-1] * (value_vertical[1:-1, 1:-1, 1:] - value_vertical[1:-1, 1:-1, :-1])
    return flux_x[:-1] - flux_x[1:] + (flux_y[:, :-1] - flux_y[:, 1:]) + (flux_z[:, :, :-1] - flux_z[:, :, 1:])

def silu_slope(pre):
    sig = jax.nn.sigmoid(pre)
    return sig * (1.0 + pre * (1.0 - sig))

def features(piece, first, shift, inside):
    lifted = padding_depth_extent(piece.astype(jnp.bfloat16))
    patches = stack_offsets(lifted, 1)
    pre = jnp.einsum('cj,jxyz->cxyz', first.astype(jnp.float32), patches.astype(jnp.float32))
    pre = pre + shift[:, None, None, None]
    feats = (jax.nn.silu(pre) * inside).astype(jnp.bfloat16)
    return (feats, lifted, pre)

def reference(noisy, weights, filter_in, bias, filter_out, upstream):
    slab = math.gcd(NX, 16)
    count = NX // slab
    starts = jnp.arange(count, dtype=jnp.int32)

    def slab_mask(s):
        xs = s * slab - 1 + jnp.arange(slab + 2, dtype=jnp.int32)
        ys = jnp.arange(NY + 2, dtype=jnp.int32) - 1
        mx = ((xs >= 0) & (xs < NX)).astype(jnp.float32)
        my = ((ys >= 0) & (ys < NY)).astype(jnp.float32)
        return mx[:, None, None] * my[None, :, None]
    pad_two = ((2, 2), (2, 2), (0, 0))
    pad_one = ((1, 1), (1, 1), (0, 0))
    fields = []
    field = noisy
    for k in range(LAYERS):
        fields.append(field)
        upad = jnp.pad(field, pad_two)

        def learned_slab(s):
            piece = lax.dynamic_slice_in_dim(upad, (s * slab).astype(jnp.int32), slab + 4, 0)
            feats, _, _ = features(piece, filter_in[k], bias[k], slab_mask(s))
            mixed = jnp.einsum('jc,cxyz->jxyz', filter_out[k].astype(jnp.float32), feats.astype(jnp.float32))
            return spread_total_sum(padding_depth_extent(mixed), 1)
        learned = lax.map(learned_slab, starts).reshape(NX, NY, NZ)
        smooth = stencil_kernel(upad[1:-1, 1:-1], jnp.pad(weights[k], pad_one))
        field = field - TAU * (field - noisy + LAMB * smooth + learned)
    cot = upstream
    data_grad = TAU * upstream * 0.0
    list_in = [None] * LAYERS
    list_out = [None] * LAYERS
    list_bias = [None] * LAYERS
    for k in reversed(range(LAYERS)):
        upad = jnp.pad(fields[k], pad_two)
        gpad = jnp.pad(cot, pad_two)

        def back_slab(s):
            start = (s * slab).astype(jnp.int32)
            piece = lax.dynamic_slice_in_dim(upad, start, slab + 4, 0)
            gpiece = lax.dynamic_slice_in_dim(gpad, start, slab + 4, 0)
            inside = slab_mask(s)
            feats, lifted, pre = features(piece, filter_in[k], bias[k], inside)
            scaled = padding_depth_extent((-TAU * gpiece).astype(jnp.bfloat16))
            shifted = stack_offsets(scaled, -1)
            dfeat = jnp.einsum('jc,jxyz->cxyz', filter_out[k].astype(jnp.float32), shifted.astype(jnp.float32))
            dfeat = dfeat * silu_slope(pre) * inside
            dfeat_b = dfeat.astype(jnp.bfloat16)
            patch_tile = stack_offsets(lifted[1:-1, 1:-1], 1)
            g_out = jnp.einsum('jxyz,cxyz->jc', shifted[:, 1:-1, 1:-1].astype(jnp.float32), feats[:, 1:-1, 1:-1].astype(jnp.float32))
            g_bias = lax.optimization_barrier(jnp.sum(dfeat[:, 1:-1, 1:-1], axis=(1, 2, 3)))
            g_in = jnp.einsum('cxyz,jxyz->cj', dfeat_b[:, 1:-1, 1:-1].astype(jnp.float32), patch_tile.astype(jnp.float32))
            back = jnp.einsum('cj,cxyz->jxyz', filter_in[k].astype(jnp.float32), dfeat_b.astype(jnp.float32))
            through = spread_total_sum(padding_depth_extent(back), -1)
            return (g_in, g_out, g_bias, through)
        g_in_all, g_out_all, g_bias_all, through = lax.map(back_slab, starts)
        through = through.reshape(NX, NY, NZ)
        smooth = stencil_kernel(gpad[1:-1, 1:-1], jnp.pad(weights[k], pad_one))
        data_grad = data_grad + TAU * cot
        cot = cot - TAU * (cot + LAMB * smooth) + through
        list_in[k] = lax.optimization_barrier(jnp.sum(g_in_all, axis=0))
        list_out[k] = lax.optimization_barrier(jnp.sum(g_out_all, axis=0))
        list_bias[k] = lax.optimization_barrier(jnp.sum(g_bias_all, axis=0))
    scale = 1.0 / math.sqrt(NX * NY * NZ)
    grad_input = cot + data_grad
    return (grad_input, jnp.stack(list_in) * scale, jnp.stack(list_out) * scale, jnp.stack(list_bias) * scale)
```

```python
import functools

import jax
import jax.numpy as jnp
from jax import lax
from jax.experimental import pallas as pl
from jax.experimental.pallas import tpu as pltpu
from jax.sharding import PartitionSpec as P

TAU = 0.15
F32 = jnp.float32
BF16 = jnp.bfloat16
MESH = pl.DeviceIdType.MESH
CH = 64
ROWS = 24
XOFF = 5
LAYERS_X = 18
SLAB = 80
DEPTH = 3 * SLAB


def iota(shape, axis):
    return lax.broadcasted_iota(jnp.int32, shape, axis)


def move_z(v, step):
    lane = iota(v.shape, 1)
    if step == 1:
        return jnp.where(lane == 127, 0.0, pltpu.roll(v, 127, 1))
    return jnp.where(lane == 0, 0.0, pltpu.roll(v, 1, 1))


def move_y(v, step):
    return pltpu.roll(v, (-step) % v.shape[0], 0)


def slab_of(v):
    ones = jnp.ones((SLAB - 3 * ROWS, 128), F32)
    return jnp.concatenate([move_z(v, -1), v, move_z(v, 1), ones], axis=0).astype(BF16)


def flux_x(v, w, i):
    return w[i] * (v[i + 1] - v[i])


def smooth_at(v, w, i):
    here, factor = v[i], w[i]
    fy = factor * (move_y(here, 1) - here)
    fz = factor * (move_z(here, 1) - here)
    return (
        flux_x(v, w, i - 1) - flux_x(v, w, i) + (move_y(fy, -1) - fy) + (move_z(fz, -1) - fz)
    )


def split_column(shape, axis):
    k = iota(shape, axis)
    sx = (k >= SLAB).astype(jnp.int32) + (k >= 2 * SLAB).astype(jnp.int32)
    rest = k - SLAB * sx
    sz = (rest >= ROWS).astype(jnp.int32) + (rest >= 2 * ROWS).astype(jnp.int32)
    row = rest - ROWS * sz
    good = (rest < 3 * ROWS) & (k < DEPTH)
    return sx, sz, row, good, rest


def split_rows(shape, axis):
    m = iota(shape, axis)
    s = sum((m >= ROWS * n).astype(jnp.int32) for n in range(1, 9))
    row = m - ROWS * s
    sx = (s >= 3).astype(jnp.int32) + (s >= 6).astype(jnp.int32)
    return sx, s - 3 * sx, row


def one_hot(hit):
    return jnp.where(hit, 1.0, 0.0).astype(BF16)


def dot(a, b):
    return jnp.dot(a, b, preferred_element_type=F32)


def dot_nt(a, b):
    return lax.dot_general(a, b, (((1,), (1,)), ((), ())), preferred_element_type=F32)


def thirds(v):
    high = v.astype(BF16)
    rest = v - high.astype(F32)
    mid = rest.astype(BF16)
    low = (rest - mid.astype(F32)).astype(BF16)
    return high, mid, low


def fill_patch(out, weight, bias_col, ys):
    shape = (32, DEPTH)
    sx, sz, row, good, _ = split_column(shape, 1)
    base = 9 * sx + sz
    j = iota(shape, 0)
    k = iota((CH, DEPTH), 1)
    extra = jnp.zeros((CH, DEPTH), F32)
    for n, part in enumerate(thirds(bias_col)):
        extra = extra + jnp.where(k == SLAB + 3 * ROWS + n, part.astype(F32), 0.0)
    for n, y in enumerate(ys):
        step = row - (y + 7)
        hit = good & (step >= 0) & (step <= 2) & (j == base + 3 * step)
        block = (dot(weight, one_hot(hit)) + extra) * 0.5
        out[n * CH : (n + 1) * CH, :] = block.astype(BF16)


def fill_spread(out, weight_t, ys):
    shape = (32, DEPTH)
    sx, sz, row, good, _ = split_column(shape, 1)
    base = 9 * (2 - sx) + (2 - sz)
    j = iota(shape, 0)
    for n, y in enumerate(ys):
        step = (y + 9) - row
        hit = good & (step >= 0) & (step <= 2) & (j == base + 3 * step)
        out[n * CH : (n + 1) * CH, :] = (dot(weight_t, one_hot(hit)) * 0.5).astype(BF16)


def fill_gather(out, weight, ys, sign, low, high):
    shape = (9 * ROWS, 32)
    sx, sz, row = split_rows(shape, 0)
    base = 9 * sx + sz
    j = iota(shape, 1)
    for n in range(0, len(ys), 2):
        halves = []
        for y in ys[n : n + 2]:
            step = (y + 9) - row if sign > 0 else row - (y + 7)
            hit = (step >= 0) & (step <= 2) & (j == base + 3 * step)
            part = one_hot(hit)
            half = dot(part, weight) if sign > 0 else dot_nt(part, weight)
            if y < 0:
                half = half * low
            elif y > 7:
                half = half * high
            halves.append(half)
        out[:, n * CH : (n + 2) * CH] = jnp.concatenate(halves, axis=1).astype(BF16)


def pair_of(stack, i):
    left = stack[pl.ds(i - 1, 3)].reshape(DEPTH, 128)
    right = stack[pl.ds(i, 3)].reshape(DEPTH, 128)
    return jnp.concatenate([left, right], axis=1)


def gather_sum(store, n, sign):
    total = None
    for sz in range(3):
        part = None
        for sx in range(3):
            at = n + sx if sign > 0 else n + 2 - sx
            lo = (3 * sx + sz) * ROWS
            term = store[at, lo : lo + ROWS, :]
            part = term if part is None else part + term
        if sz != 1:
            part = move_z(part, sign * (sz - 1))
        total = part if total is None else total + part
    return total


def fold_rows(out):
    total = out[0:CH]
    for y in range(1, 8):
        total = total + pltpu.roll(out[y * CH : (y + 1) * CH], 256 - y, 1)
    return total


def pick_columns(layer, first):
    shape = (256, 128)
    sx, sz, row, good, rest = split_column(shape, 0)
    lane = iota(shape, 1)
    if first:
        step = row - 7
        j = 9 * sx + 3 * step + sz
        ok = good & (step >= 0) & (step <= 2)
        hit = ok & (lane == 64 * layer + j)
        spare = (sx == 1) & (rest == 3 * ROWS) & (lane == 64 * layer + 27)
        return one_hot(hit | spare)
    step = 9 - row
    j = 9 * (2 - sx) + 3 * step + (2 - sz)
    ok = good & (step >= 0) & (step <= 2)
    return one_hot(ok & (lane == 64 * layer + 32 + j))


def packed_sums(out, layer, first):
    folded = fold_rows(out)
    pick = pick_columns(layer, first)
    high, mid, low = thirds(folded)
    return dot(high, pick) + dot(mid, pick) + dot(low, pick)


def layers_beside(stack):
    parts = [stack[i - 1 : i + 2].reshape(DEPTH, 128) for i in range(XOFF, XOFF + 8)]
    whole = jnp.concatenate(parts, axis=1)
    return jnp.concatenate([whole, jnp.zeros((256 - DEPTH, 1024), BF16)], axis=0)


def kernel(
    size_x, size_y,
    noisy, weights, filter_in, bias, filter_out, upstream,
    out_grad, out_w1, out_w2, out_b,
    send_x, send_yl, send_yh, got_x, got_y,
    u0, g0, w0, w1, u1, g1,
    su0, ss1, su1, ss0,
    t1a, t1b, t2b, t2a, toa, t3b, t3a,
    pad_in, pad_out,
    qbuf, pbuf, h0, d0, h1, dab1, dab0,
    ring_x, ring_y, ring_c, back_x, back_y, back_c, part,
    pack, red_g, red_y, red_z, tile_y, tile_z, tile_f, final,
    halo_send, halo_recv, ring_send, ring_recv, red_send, red_recv,
):
    gx, gy = lax.axis_index("gx"), lax.axis_index("gy")
    core, xlo, py = lax.rem(gx, 2), lax.rem(gx // 2, 2), gx // 4
    xhi, pz = lax.rem(gy, 2), gy // 2
    ny, nz = size_x // 4, size_y // 2
    me_g = (xhi * 2 + xlo) * 2 + core

    def near(dx, dy):
        return (lax.rem(gx + dx + size_x, size_x), lax.rem(gy + dy + size_y, size_y))

    def in_group(step):
        to = lax.rem(me_g + step, 8)
        c, x = lax.rem(to, 2), to // 2
        return to, (py * 4 + lax.rem(x, 2) * 2 + c, pz * 2 + x // 2)

    def along_y(step):
        return (lax.rem(py + step, ny) * 4 + xlo * 2 + core, gy)

    def along_z(step):
        return (gx, lax.rem(pz + step, nz) * 2 + xhi)

    sides = [(dx, dy) for dx in (-1, 0, 1) for dy in (-1, 0, 1) if (dx, dy) != (0, 0)]
    barrier = pltpu.get_barrier_semaphore()
    peers = [near(*side) for side in sides] + [in_group(s)[1] for s in range(1, 8)]
    peers += [along_y(s) for s in range(1, ny)] + [along_z(s) for s in range(1, nz)]
    for peer in peers:
        pl.semaphore_signal(barrier, inc=1, device_id=peer, device_id_type=MESH)

    mxl = jnp.where(gx > 0, 1.0, 0.0).astype(F32)
    mxh = jnp.where(gx < size_x - 1, 1.0, 0.0).astype(F32)
    myl = jnp.where(gy > 0, 1.0, 0.0).astype(F32)
    myh = jnp.where(gy < size_y - 1, 1.0, 0.0).astype(F32)

    row8 = iota((8, 128), 0)
    for x in range(8):
        u, g, wa, wb = noisy[x], upstream[x], weights[0, x], weights[1, x]
        send_x[x] = jnp.concatenate([u, g, wa, wb], axis=0).astype(BF16)
        top = jnp.where(row8 < 5, pltpu.roll(u, 5, 0), g)
        low = jnp.where(row8 < 4, pltpu.roll(wa, 4, 0), pltpu.roll(wb, 6, 0))
        send_yl[x] = jnp.concatenate([top, low], axis=0).astype(BF16)
        top = jnp.where(row8 < 5, u, pltpu.roll(g, 5, 0))
        low = jnp.where(row8 < 4, wa, pltpu.roll(wb, 4, 0))
        send_yh[x] = jnp.concatenate([top, low], axis=0).astype(BF16)
    pl.semaphore_wait(barrier, len(peers))

    halo = []
    span = {-1: (0, 13), 0: (0, 5), 1: (3, 0)}
    for n, (dx, dy) in enumerate(sides):
        start, land = span[dx]
        if dy == 0:
            src, dst = send_x.at[pl.ds(start, 5)], got_x.at[0 if dx > 0 else 1]
        else:
            count = 8 if dx == 0 else 5
            src = (send_yl if dy > 0 else send_yh).at[pl.ds(start, count)]
            dst = got_y.at[0 if dy > 0 else 1, pl.ds(land, count)]
        copy = pltpu.make_async_remote_copy(
            src_ref=src, dst_ref=dst, send_sem=halo_send.at[n], recv_sem=halo_recv.at[n],
            device_id=near(dx, dy), device_id_type=MESH,
        )
        copy.start()
        halo.append(copy)

    eye = iota((CH, CH), 0) == iota((CH, CH), 1)
    pad_in[...] = jnp.zeros_like(pad_in)
    pad_out[...] = jnp.zeros_like(pad_out)
    cols = []
    for k in range(2):
        pad_in[k, :, 0:27] = filter_in[k].astype(F32)
        pad_out[k, 0:27, :] = filter_out[k].astype(F32)
        spread = jnp.broadcast_to(bias[k : k + 1, :], (CH, CH))
        cols.append(jnp.sum(jnp.where(eye, spread, 0.0), axis=1, keepdims=True))
    win = [pad_in[k, :, 0:32].astype(BF16) for k in range(2)]
    wout = [pad_out[k].astype(BF16) for k in range(2)]
    wout_t = [dot_nt(one_hot(eye), wout[k]).astype(BF16) for k in range(2)]
    fill_patch(t1a, win[0], cols[0], range(-4, 12))
    fill_gather(toa, wout[0], range(-4, 12), 1, myl, myh)
    fill_patch(t1b, win[1], cols[1], range(-2, 10))
    fill_spread(t2b, wout_t[1], range(-2, 10))
    fill_gather(t3b, win[1], range(-2, 10), -1, myl, myh)
    fill_spread(t2a, wout_t[0], range(0, 8))
    fill_gather(t3a, win[0], range(0, 8), -1, myl, myh)

    for copy in halo:
        copy.wait()

    for i in range(LAYERS_X):
        if i < XOFF:
            rows, edge = got_x[0, i].astype(F32) * mxl, mxl
        elif i >= XOFF + 8:
            rows, edge = got_x[1, i - XOFF - 8].astype(F32) * mxh, mxh
        else:
            x, edge = i - XOFF, jnp.float32(1.0)
            rows = jnp.concatenate([noisy[x], upstream[x], weights[0, x], weights[1, x]], axis=0)
        lo = got_y[0, i].astype(F32) * (edge * myl)
        hi = got_y[1, i].astype(F32) * (edge * myh)
        lo_t, lo_b, hi_t, hi_b = lo[0:8], lo[8:16], hi[0:8], hi[8:16]
        u = jnp.concatenate([pltpu.roll(lo_t, 3, 0), rows[0:8], hi_t], axis=0)
        u0[i] = u
        su0[i] = slab_of(u)
        w0[i] = jnp.concatenate([pltpu.roll(lo_b, 4, 0), rows[16:24], hi_b], axis=0)
        if 2 <= i < 16:
            g = jnp.concatenate([lo_t, rows[8:16], pltpu.roll(hi_t, 3, 0)], axis=0)
            g0[i] = g
            ss1[i] = slab_of(-TAU * g)
            w1[i] = jnp.concatenate(
                [pltpu.roll(lo_b, 2, 0), rows[24:32], pltpu.roll(hi_b, 4, 0)], axis=0
            )

    row24 = iota((ROWS, 128), 0)
    inside_y = jnp.where(row24 < 8, myl, jnp.where(row24 < 16, 1.0, myh))

    def x_mask(i):
        return jnp.where(i < XOFF, mxl, jnp.where(i >= XOFF + 8, mxh, 1.0))

    def forward(p, keep):
        i = 1 + 2 * p
        half = dot(t1a[...], pair_of(su0, i))
        t = jnp.tanh(half)
        h = half + half * t
        hb = h.astype(BF16)
        if keep:
            tile = slice(4 * CH, 12 * CH)
            h0[p - 2] = hb[tile]
            d0[p - 2] = (1.0 + t[tile]) + (h[tile] - h[tile] * t[tile])
        q = dot(toa[...], hb)
        qbuf[2 * p] = q[:, 0:128] * x_mask(i)
        qbuf[2 * p + 1] = q[:, 128:256] * x_mask(i + 1)

    @pl.loop(0, 4)
    def _(n):
        forward(jnp.where(n < 2, n, n + 4), False)

    @pl.loop(2, 6)
    def _(p):
        forward(p, True)

    for i in range(2, 16):
        learned = gather_sum(qbuf, i - 2, 1)
        v = u0[i] - TAU * (smooth_at(u0, w0, i) + learned)
        v = v * inside_y
        if i < XOFF:
            v = v * mxl
        elif i >= XOFF + 8:
            v = v * mxh
        su1[i] = slab_of(v)

    def middle(p, keep):
        i = 3 + 2 * p
        half = dot(t1b[...], pair_of(su1, i))
        dh = dot(t2b[...], pair_of(ss1, i))
        t = jnp.tanh(half)
        h = half + half * t
        dab = (dh * ((1.0 + t) + (h - h * t))).astype(BF16)
        if keep:
            tile = slice(2 * CH, 10 * CH)
            h1[p - 1] = h[tile].astype(BF16)
            dab1[p - 1] = dab[tile]
        q = dot(t3b[...], dab)
        pbuf[2 * p] = q[:, 0:128] * x_mask(i)
        pbuf[2 * p + 1] = q[:, 128:256] * x_mask(i + 1)

    @pl.loop(0, 2)
    def _(n):
        middle(n * 5, False)

    @pl.loop(1, 5)
    def _(p):
        middle(p, True)

    for i in range(4, 14):
        g = g0[i]
        v = g - TAU * (g + smooth_at(g0, w1, i)) + gather_sum(pbuf, i - 4, -1)
        v = v * inside_y
        if i < XOFF:
            v = v * mxl
        elif i >= XOFF + 8:
            v = v * mxh
        g1[i] = v
        ss0[i] = slab_of(-TAU * v)

    @pl.loop(0, 4)
    def _(p):
        dh = dot(t2a[...], pair_of(ss0, XOFF + 2 * p))
        dab0[p] = (dh * d0[p]).astype(BF16)

    def beside(store):
        return jnp.concatenate([store[p] for p in range(4)], axis=1)

    sums = packed_sums(dot_nt(beside(h0), layers_beside(ss0)), 0, False)
    sums = sums + packed_sums(dot_nt(beside(dab0), layers_beside(su0)), 0, True)
    sums = sums + packed_sums(dot_nt(beside(h1), layers_beside(ss1)), 1, False)
    sums = sums + packed_sums(dot_nt(beside(dab1), layers_beside(su1)), 1, True)
    for n in range(8):
        pack[n] = sums[8 * n : 8 * n + 8]

    first = []
    for s in range(1, 8):
        to, peer = in_group(s)
        copy = pltpu.make_async_remote_copy(
            src_ref=pack.at[to], dst_ref=red_g.at[me_g],
            send_sem=red_send.at[0, s], recv_sem=red_recv.at[0, s],
            device_id=peer, device_id_type=MESH,
        )
        copy.start()
        first.append(copy)
    red_g[me_g] = pack[me_g]

    pbuf[0] = jnp.zeros_like(pbuf[0])
    pbuf[1] = jnp.zeros_like(pbuf[1])
    pbuf[10] = jnp.zeros_like(pbuf[0])
    pbuf[11] = jnp.zeros_like(pbuf[0])

    @pl.loop(0, 4)
    def _(p):
        q = dot(t3a[...], dab0[p])
        pbuf[2 * p + 2] = q[:, 0:128]
        pbuf[2 * p + 3] = q[:, 128:256]

    for n in range(10):
        part[n] = gather_sum(pbuf, n, -1)
    ring_x[0] = part[0, 8:16, :]
    ring_x[1] = part[9, 8:16, :]
    for side, row in ((0, 7), (1, 16)):
        ring_y[side] = jnp.concatenate([part[n, row : row + 1, :] for n in range(1, 9)], axis=0)
        for end, n in ((0, 0), (1, 9)):
            ring_c[end, side] = jnp.broadcast_to(part[n, row : row + 1, :], (8, 128))

    around = []
    for n, (dx, dy) in enumerate(sides):
        a, b = (0 if dx < 0 else 1), (0 if dy < 0 else 1)
        if dy == 0:
            src, dst = ring_x.at[a], back_x.at[a]
        elif dx == 0:
            src, dst = ring_y.at[b], back_y.at[b]
        else:
            src, dst = ring_c.at[a, b], back_c.at[a, b]
        copy = pltpu.make_async_remote_copy(
            src_ref=src, dst_ref=dst, send_sem=ring_send.at[n], recv_sem=ring_recv.at[n],
            device_id=near(dx, dy), device_id_type=MESH,
        )
        copy.start()
        around.append(copy)

    for copy in first:
        copy.wait()
    tile_y[...] = sum_slots(red_g)

    second = []
    for s in range(1, ny):
        copy = pltpu.make_async_remote_copy(
            src_ref=tile_y, dst_ref=red_y.at[py],
            send_sem=red_send.at[1, s], recv_sem=red_recv.at[1, s],
            device_id=along_y(s), device_id_type=MESH,
        )
        copy.start()
        second.append(copy)
    red_y[py] = tile_y[...]

    for copy in around:
        copy.wait()
    for x in range(8):
        i = x + XOFF
        back = part[x + 1, 8:16, :]
        add_lo = back_y[1, x : x + 1, :] * myl
        add_hi = back_y[0, x : x + 1, :] * myh
        if x == 0:
            back = back + back_x[1] * mxl
            add_lo = add_lo + back_c[1, 1, 0:1, :] * (mxl * myl)
            add_hi = add_hi + back_c[1, 0, 0:1, :] * (mxl * myh)
        if x == 7:
            back = back + back_x[0] * mxh
            add_lo = add_lo + back_c[0, 1, 0:1, :] * (mxh * myl)
            add_hi = add_hi + back_c[0, 0, 0:1, :] * (mxh * myh)
        back = back + jnp.where(row8 == 0, add_lo, 0.0) + jnp.where(row8 == 7, add_hi, 0.0)
        smooth = smooth_at(g1, w0, i)[8:16]
        out_grad[x] = g1[i, 8:16, :] - TAU * smooth + back + TAU * upstream[x]

    for copy in second:
        copy.wait()
    tile_z[...] = sum_slots(red_y)
    third = []
    for s in range(1, nz):
        copy = pltpu.make_async_remote_copy(
            src_ref=tile_z, dst_ref=red_z.at[pz],
            send_sem=red_send.at[2, s], recv_sem=red_recv.at[2, s],
            device_id=along_z(s), device_id_type=MESH,
        )
        copy.start()
        third.append(copy)
    red_z[pz] = tile_z[...]
    for copy in third:
        copy.wait()
    tile_f[...] = sum_slots(red_z)
    fourth = []
    for s in range(1, 8):
        to, peer = in_group(s)
        copy = pltpu.make_async_remote_copy(
            src_ref=tile_f, dst_ref=final.at[me_g],
            send_sem=red_send.at[3, s], recv_sem=red_recv.at[3, s],
            device_id=peer, device_id_type=MESH,
        )
        copy.start()
        fourth.append(copy)
    final[me_g] = tile_f[...]
    for copy in fourth:
        copy.wait()

    scale = 1.0 / 2048.0
    whole = final[...].reshape(CH, 128) * scale
    turned = whole.T
    for k in range(2):
        out_w1[k] = whole[:, 64 * k : 64 * k + 27]
        out_w2[k] = turned[64 * k + 32 : 64 * k + 59, :]
        out_b[k : k + 1, :] = turned[64 * k + 27 : 64 * k + 28, :]


def sum_slots(store):
    total = store[0]
    for n in range(1, store.shape[0]):
        total = total + store[n]
    return total


def body(noisy, weights, filter_in, bias, filter_out, upstream):
    size_x, size_y = lax.axis_size("gx"), lax.axis_size("gy")
    field = pltpu.VMEM((LAYERS_X, ROWS, 128), F32)
    stack = pltpu.VMEM((LAYERS_X, SLAB, 128), BF16)
    vm = lambda *shape: pltpu.VMEM(shape, F32)
    vb = lambda *shape: pltpu.VMEM(shape, BF16)
    dma = lambda *shape: pltpu.SemaphoreType.DMA(shape)
    scratch = [
        vb(8, 32, 128), vb(8, 16, 128), vb(8, 16, 128), vb(2, 5, 32, 128), vb(2, LAYERS_X, 16, 128),
        field, field, field, field, field, field,
        stack, stack, stack, stack,
        vb(16 * CH, DEPTH), vb(12 * CH, DEPTH), vb(12 * CH, DEPTH), vb(8 * CH, DEPTH),
        vb(9 * ROWS, 16 * CH), vb(9 * ROWS, 12 * CH), vb(9 * ROWS, 8 * CH),
        vm(2, CH, 128), vm(2, 32, CH),
        vm(16, 9 * ROWS, 128), vm(12, 9 * ROWS, 128),
        vb(4, 8 * CH, 256), vm(4, 8 * CH, 256), vb(4, 8 * CH, 256), vb(4, 8 * CH, 256), vb(4, 8 * CH, 256),
        vm(2, 8, 128), vm(2, 8, 128), vm(2, 2, 8, 128), vm(2, 8, 128), vm(2, 8, 128), vm(2, 2, 8, 128), vm(10, ROWS, 128),
        vm(8, 8, 128), vm(8, 8, 128), vm(size_x // 4, 8, 128), vm(size_y // 2, 8, 128),
        vm(8, 128), vm(8, 128), vm(8, 128), vm(8, 8, 128),
        dma(8), dma(8), dma(8), dma(8), dma(4, 8), dma(4, 8),
    ]
    spec = pl.BlockSpec(memory_space=pltpu.VMEM)
    return pl.pallas_call(
        functools.partial(kernel, size_x, size_y),
        out_shape=(
            jax.ShapeDtypeStruct((8, 8, 128), F32),
            jax.ShapeDtypeStruct((2, CH, 27), F32),
            jax.ShapeDtypeStruct((2, 27, CH), F32),
            jax.ShapeDtypeStruct((2, CH), F32),
        ),
        in_specs=[spec] * 6,
        out_specs=(spec,) * 4,
        scratch_shapes=scratch,
        compiler_params=pltpu.CompilerParams(
            collective_id=0, has_side_effects=True, vmem_limit_bytes=48 * 1024 * 1024
        ),
    )(noisy, weights, filter_in, bias, filter_out, upstream)


def solution(mesh):
    return jax.shard_map(
        body,
        mesh=mesh,
        in_specs=(
            P("gx", "gy", None),
            P(None, "gx", "gy", None),
            P(),
            P(),
            P(),
            P("gx", "gy", None),
        ),
        out_specs=(P("gx", "gy", None), P(), P(), P()),
        check_vma=False,
    )
```

```python
import functools

import jax
import jax.numpy as jnp
from jax import lax
from jax.experimental import pallas as pl
from jax.experimental.pallas import tpu as pltpu
from jax.sharding import PartitionSpec as P

TAU = 0.15
F32 = jnp.float32
BF16 = jnp.bfloat16
MESH = pl.DeviceIdType.MESH
CH = 64
ROWS = 24
XOFF = 5
LAYERS_X = 18
SLAB = 80
DEPTH = 3 * SLAB
GROWS = 16
GBASE = 4


def iota(shape, axis):
    return lax.broadcasted_iota(jnp.int32, shape, axis)


def move_z(v, step):
    lane = iota(v.shape, 1)
    if step == 1:
        return jnp.where(lane == 127, 0.0, pltpu.roll(v, 127, 1))
    return jnp.where(lane == 0, 0.0, pltpu.roll(v, 1, 1))


def move_y(v, step):
    return pltpu.roll(v, (-step) % v.shape[0], 0)


def slab_of(v):
    ones = jnp.ones((SLAB - 3 * ROWS, 128), F32)
    return jnp.concatenate([move_z(v, -1), v, move_z(v, 1), ones], axis=0).astype(BF16)


def flux_x(v, w, i):
    return w[i] * (v[i + 1] - v[i])


def smooth_at(v, w, i):
    here, factor = v[i], w[i]
    fy = factor * (move_y(here, 1) - here)
    fz = factor * (move_z(here, 1) - here)
    return (
        flux_x(v, w, i - 1) - flux_x(v, w, i) + (move_y(fy, -1) - fy) + (move_z(fz, -1) - fz)
    )


def split_column(shape, axis):
    k = iota(shape, axis)
    sx = (k >= SLAB).astype(jnp.int32) + (k >= 2 * SLAB).astype(jnp.int32)
    rest = k - SLAB * sx
    sz = (rest >= ROWS).astype(jnp.int32) + (rest >= 2 * ROWS).astype(jnp.int32)
    row = rest - ROWS * sz
    good = (rest < 3 * ROWS) & (k < DEPTH)
    return sx, sz, row, good, rest


def split_rows(shape, axis):
    m = iota(shape, axis)
    s = sum((m >= GROWS * n).astype(jnp.int32) for n in range(1, 9))
    row = m - GROWS * s + GBASE
    sx = (s >= 3).astype(jnp.int32) + (s >= 6).astype(jnp.int32)
    return sx, s - 3 * sx, row


def one_hot(hit):
    return jnp.where(hit, 1.0, 0.0).astype(BF16)


def dot(a, b):
    return jnp.dot(a, b, preferred_element_type=F32)


def dot_nt(a, b):
    return lax.dot_general(a, b, (((1,), (1,)), ((), ())), preferred_element_type=F32)


def thirds(v):
    high = v.astype(BF16)
    rest = v - high.astype(F32)
    mid = rest.astype(BF16)
    low = (rest - mid.astype(F32)).astype(BF16)
    return high, mid, low


def fill_patch(out, weight, bias_col, ys):
    shape = (32, DEPTH)
    sx, sz, row, good, _ = split_column(shape, 1)
    base = 9 * sx + sz
    j = iota(shape, 0)
    k = iota((CH, DEPTH), 1)
    extra = jnp.zeros((CH, DEPTH), F32)
    for n, part in enumerate(thirds(bias_col)):
        extra = extra + jnp.where(k == SLAB + 3 * ROWS + n, part.astype(F32), 0.0)
    for n, y in enumerate(ys):
        step = row - (y + 7)
        hit = good & (step >= 0) & (step <= 2) & (j == base + 3 * step)
        block = (dot(weight, one_hot(hit)) + extra) * 0.5
        out[n * CH : (n + 1) * CH, :] = block.astype(BF16)


def fill_spread(out, weight_t, ys):
    shape = (32, DEPTH)
    sx, sz, row, good, _ = split_column(shape, 1)
    base = 9 * (2 - sx) + (2 - sz)
    j = iota(shape, 0)
    for n, y in enumerate(ys):
        step = (y + 9) - row
        hit = good & (step >= 0) & (step <= 2) & (j == base + 3 * step)
        out[n * CH : (n + 1) * CH, :] = (dot(weight_t, one_hot(hit)) * 0.5).astype(BF16)


def fill_gather(out, weight, ys, sign, low, high):
    shape = (9 * GROWS, 32)
    sx, sz, row = split_rows(shape, 0)
    base = 9 * sx + sz
    j = iota(shape, 1)
    for n in range(0, len(ys), 2):
        halves = []
        for y in ys[n : n + 2]:
            step = (y + 9) - row if sign > 0 else row - (y + 7)
            hit = (step >= 0) & (step <= 2) & (j == base + 3 * step)
            part = one_hot(hit)
            half = dot(part, weight)
            if y < 0:
                half = half * low
            elif y > 7:
                half = half * high
            halves.append(half)
        out[:, n * CH : (n + 2) * CH] = jnp.concatenate(halves, axis=1).astype(BF16)


def pair_of(stack, i):
    left = stack[pl.ds(i - 1, 3)].reshape(DEPTH, 128)
    right = stack[pl.ds(i, 3)].reshape(DEPTH, 128)
    return jnp.concatenate([left, right], axis=1)


def gather_sum(store, n, sign):
    total = None
    for sz in range(3):
        part = None
        for sx in range(3):
            at = n + sx if sign > 0 else n + 2 - sx
            lo = (3 * sx + sz) * GROWS
            term = store[at, lo : lo + GROWS, :]
            part = term if part is None else part + term
        if sz != 1:
            part = move_z(part, sign * (sz - 1))
        total = part if total is None else total + part
    pad = jnp.zeros((GBASE, 128), F32)
    return jnp.concatenate([pad, total, pad], axis=0)


def fold_rows(out):
    total = out[0:CH]
    for y in range(1, 8):
        total = total + pltpu.roll(out[y * CH : (y + 1) * CH], 256 - y, 1)
    return total


def pick_columns(layer, first):
    shape = (256, 128)
    sx, sz, row, good, rest = split_column(shape, 0)
    lane = iota(shape, 1)
    if first:
        step = row - 7
        j = 9 * sx + 3 * step + sz
        ok = good & (step >= 0) & (step <= 2)
        hit = ok & (lane == 64 * layer + j)
        spare = (sx == 1) & (rest == 3 * ROWS) & (lane == 64 * layer + 27)
        return one_hot(hit | spare)
    step = 9 - row
    j = 9 * (2 - sx) + 3 * step + (2 - sz)
    ok = good & (step >= 0) & (step <= 2)
    return one_hot(ok & (lane == 64 * layer + 32 + j))


def packed_sums(out, layer, first):
    folded = fold_rows(out)
    pick = pick_columns(layer, first)
    high, mid, low = thirds(folded)
    return dot(high, pick) + dot(mid, pick) + dot(low, pick)


def layers_beside(stack):
    parts = [stack[i - 1 : i + 2].reshape(DEPTH, 128) for i in range(XOFF, XOFF + 8)]
    whole = jnp.concatenate(parts, axis=1)
    return jnp.concatenate([whole, jnp.zeros((256 - DEPTH, 1024), BF16)], axis=0)


def kernel(
    size_x, size_y,
    noisy_at, weights_at, filter_in_at, bias_at, filter_out_at, upstream_at,
    out_grad, out_w1, out_w2, out_b,
    noisy, weights, filter_in, bias, filter_out, upstream,
    send_x, send_yl, send_yh, got_x, got_y,
    u0, g0, w0, w1, u1, g1,
    su0, ss1, su1, ss0,
    t1a, t1b, t2b, t2a, toa, t3b, t3a,
    pad_in, pad_out,
    qbuf, pbuf, h0, d0, h1, dab1, dab0,
    ring_x, ring_y, ring_c, back_x, back_y, back_c, part,
    pack, red_g, red_y, red_z, tile_y, tile_z, tile_f, final,
    fetch_sem, halo_send, halo_recv, ring_send, ring_recv, red_send, red_recv,
):
    gx, gy = lax.axis_index("gx"), lax.axis_index("gy")
    core, xlo, py = lax.rem(gx, 2), lax.rem(gx // 2, 2), gx // 4
    xhi, pz = lax.rem(gy, 2), gy // 2
    ny, nz = size_x // 4, size_y // 2
    me_g = (xhi * 2 + xlo) * 2 + core

    def near(dx, dy):
        return (lax.rem(gx + dx + size_x, size_x), lax.rem(gy + dy + size_y, size_y))

    def in_group(step):
        to = lax.rem(me_g + step, 8)
        c, x = lax.rem(to, 2), to // 2
        return to, (py * 4 + lax.rem(x, 2) * 2 + c, pz * 2 + x // 2)

    def along_y(step):
        return (lax.rem(py + step, ny) * 4 + xlo * 2 + core, gy)

    def along_z(step):
        return (gx, lax.rem(pz + step, nz) * 2 + xhi)

    sides = [(-1, -1), (1, 1), (-1, 1), (1, -1), (0, -1), (0, 1), (-1, 0), (1, 0)]
    far_first = (4, 3, 5, 2, 6, 1, 7)
    barrier = pltpu.get_barrier_semaphore()
    peers = [near(*side) for side in sides] + [in_group(s)[1] for s in range(1, 8)]
    peers += [along_y(s) for s in range(1, ny)] + [along_z(s) for s in range(1, nz)]
    for peer in peers:
        pl.semaphore_signal(barrier, inc=1, device_id=peer, device_id_type=MESH)

    fetched = [
        pltpu.make_async_copy(src, dst, fetch_sem.at[n])
        for n, (src, dst) in enumerate((
            (noisy_at, noisy), (upstream_at, upstream), (weights_at, weights),
            (filter_in_at, filter_in), (filter_out_at, filter_out), (bias_at, bias),
        ))
    ]
    for copy in fetched:
        copy.start()

    mxl = jnp.where(gx > 0, 1.0, 0.0).astype(F32)
    mxh = jnp.where(gx < size_x - 1, 1.0, 0.0).astype(F32)
    myl = jnp.where(gy > 0, 1.0, 0.0).astype(F32)
    myh = jnp.where(gy < size_y - 1, 1.0, 0.0).astype(F32)

    row8 = iota((8, 128), 0)
    for copy in fetched[:3]:
        copy.wait()
    for x in range(8):
        u, g, wa, wb = noisy[x], upstream[x], weights[0, x], weights[1, x]
        send_x[x] = jnp.concatenate([u, g, wa, wb], axis=0).astype(BF16)
        top = jnp.where(row8 < 5, pltpu.roll(u, 5, 0), g)
        low = jnp.where(row8 < 4, pltpu.roll(wa, 4, 0), pltpu.roll(wb, 6, 0))
        send_yl[x] = jnp.concatenate([top, low], axis=0).astype(BF16)
        top = jnp.where(row8 < 5, u, pltpu.roll(g, 5, 0))
        low = jnp.where(row8 < 4, wa, pltpu.roll(wb, 4, 0))
        send_yh[x] = jnp.concatenate([top, low], axis=0).astype(BF16)
    pl.semaphore_wait(barrier, len(peers))

    halo = []
    span = {-1: (0, 13), 0: (0, 5), 1: (3, 0)}
    for n, (dx, dy) in enumerate(sides):
        start, land = span[dx]
        if dy == 0:
            src, dst = send_x.at[pl.ds(start, 5)], got_x.at[0 if dx > 0 else 1]
        else:
            count = 8 if dx == 0 else 5
            src = (send_yl if dy > 0 else send_yh).at[pl.ds(start, count)]
            dst = got_y.at[0 if dy > 0 else 1, pl.ds(land, count)]
        copy = pltpu.make_async_remote_copy(
            src_ref=src, dst_ref=dst, send_sem=halo_send.at[n], recv_sem=halo_recv.at[n],
            device_id=near(dx, dy), device_id_type=MESH,
        )
        copy.start()
        halo.append(copy)

    eye = iota((CH, CH), 0) == iota((CH, CH), 1)
    for copy in fetched[3:]:
        copy.wait()
    pad_in[...] = jnp.zeros_like(pad_in)
    pad_out[...] = jnp.zeros_like(pad_out)
    whole_in, whole_out = filter_in[...].astype(F32), filter_out[...].astype(F32)
    cols = []
    for k in range(2):
        pad_in[k, 0:27, :] = whole_in[:, k, :]
        pad_out[k, 0:27, :] = whole_out[:, k, :]
        spread = jnp.broadcast_to(bias[k : k + 1, :], (CH, CH))
        cols.append(jnp.sum(jnp.where(eye, spread, 0.0), axis=1, keepdims=True))
    win_t = [pad_in[k].astype(BF16) for k in range(2)]
    wout = [pad_out[k].astype(BF16) for k in range(2)]
    win = [dot_nt(one_hot(eye), win_t[k]).astype(BF16) for k in range(2)]
    wout_t = [dot_nt(one_hot(eye), wout[k]).astype(BF16) for k in range(2)]
    fill_patch(t1a, win[0], cols[0], range(-4, 12))
    fill_gather(toa, wout[0], range(-4, 12), 1, myl, myh)
    fill_patch(t1b, win[1], cols[1], range(-2, 10))
    fill_spread(t2b, wout_t[1], range(-2, 10))
    fill_gather(t3b, win_t[1], range(-2, 10), -1, myl, myh)
    fill_spread(t2a, wout_t[0], range(0, 8))
    fill_gather(t3a, win_t[0], range(0, 8), -1, myl, myh)

    for copy in halo:
        copy.wait()

    for i in range(LAYERS_X):
        if i < XOFF:
            rows, edge = got_x[0, i].astype(F32) * mxl, mxl
        elif i >= XOFF + 8:
            rows, edge = got_x[1, i - XOFF - 8].astype(F32) * mxh, mxh
        else:
            x, edge = i - XOFF, jnp.float32(1.0)
            rows = jnp.concatenate([noisy[x], upstream[x], weights[0, x], weights[1, x]], axis=0)
        lo = got_y[0, i].astype(F32) * (edge * myl)
        hi = got_y[1, i].astype(F32) * (edge * myh)
        lo_t, lo_b, hi_t, hi_b = lo[0:8], lo[8:16], hi[0:8], hi[8:16]
        u = jnp.concatenate([pltpu.roll(lo_t, 3, 0), rows[0:8], hi_t], axis=0)
        u0[i] = u
        su0[i] = slab_of(u)
        w0[i] = jnp.concatenate([pltpu.roll(lo_b, 4, 0), rows[16:24], hi_b], axis=0)
        if 2 <= i < 16:
            g = jnp.concatenate([lo_t, rows[8:16], pltpu.roll(hi_t, 3, 0)], axis=0)
            g0[i] = g
            ss1[i] = slab_of(-TAU * g)
            w1[i] = jnp.concatenate(
                [pltpu.roll(lo_b, 2, 0), rows[24:32], pltpu.roll(hi_b, 4, 0)], axis=0
            )

    row24 = iota((ROWS, 128), 0)
    inside_y = jnp.where(row24 < 8, myl, jnp.where(row24 < 16, 1.0, myh))

    def x_mask(i):
        return jnp.where(i < XOFF, mxl, jnp.where(i >= XOFF + 8, mxh, 1.0))

    def forward(p, keep):
        i = 1 + 2 * p
        rhs = pair_of(su0, i)
        q = None
        for m in range(4):
            cut = slice(4 * CH * m, 4 * CH * (m + 1))
            half = dot(t1a[cut, :], rhs)
            t = jnp.tanh(half)
            h = half + half * t
            hb = h.astype(BF16)
            if keep and m in (1, 2):
                own = slice(4 * CH * (m - 1), 4 * CH * m)
                h0[p - 2, own, :] = hb
                d0[p - 2, own, :] = (1.0 + t) + (h - h * t)
            term = dot(toa[:, cut], hb)
            q = term if q is None else q + term
        qbuf[2 * p] = q[:, 0:128] * x_mask(i)
        qbuf[2 * p + 1] = q[:, 128:256] * x_mask(i + 1)

    @pl.loop(0, 4, unroll=2)
    def _(n):
        forward(jnp.where(n < 2, n, n + 4), False)

    @pl.loop(2, 6, unroll=2)
    def _(p):
        forward(p, True)

    for i in range(2, 16):
        learned = gather_sum(qbuf, i - 2, 1)
        v = u0[i] - TAU * (smooth_at(u0, w0, i) + learned)
        v = v * inside_y
        if i < XOFF:
            v = v * mxl
        elif i >= XOFF + 8:
            v = v * mxh
        su1[i] = slab_of(v)

    def middle(p, keep):
        i = 3 + 2 * p
        rhs_u, rhs_s = pair_of(su1, i), pair_of(ss1, i)
        q = None
        for first, last in ((0, 2), (2, 6), (6, 10), (10, 12)):
            cut = slice(CH * first, CH * last)
            half = dot(t1b[cut, :], rhs_u)
            dh = dot(t2b[cut, :], rhs_s)
            t = jnp.tanh(half)
            h = half + half * t
            dab = (dh * ((1.0 + t) + (h - h * t))).astype(BF16)
            if keep and last - first == 4:
                own = slice(CH * (first - 2), CH * (last - 2))
                h1[p - 1, own, :] = h.astype(BF16)
                dab1[p - 1, own, :] = dab
            term = dot(t3b[:, cut], dab)
            q = term if q is None else q + term
        pbuf[2 * p] = q[:, 0:128] * x_mask(i)
        pbuf[2 * p + 1] = q[:, 128:256] * x_mask(i + 1)

    @pl.loop(0, 2, unroll=2)
    def _(n):
        middle(n * 5, False)

    @pl.loop(1, 5, unroll=2)
    def _(p):
        middle(p, True)

    def beside(store):
        return jnp.concatenate([store[p] for p in range(4)], axis=1)

    sums = packed_sums(dot_nt(beside(h1), layers_beside(ss1)), 1, False)
    sums = sums + packed_sums(dot_nt(beside(dab1), layers_beside(su1)), 1, True)

    for i in range(4, 14):
        g = g0[i]
        v = g - TAU * (g + smooth_at(g0, w1, i)) + gather_sum(pbuf, i - 4, -1)
        v = v * inside_y
        if i < XOFF:
            v = v * mxl
        elif i >= XOFF + 8:
            v = v * mxh
        g1[i] = v
        ss0[i] = slab_of(-TAU * v)

    @pl.loop(0, 4, unroll=4)
    def _(p):
        dh = dot(t2a[...], pair_of(ss0, XOFF + 2 * p))
        dab0[p] = (dh * d0[p]).astype(BF16)

    sums = sums + packed_sums(dot_nt(beside(h0), layers_beside(ss0)), 0, False)
    sums = sums + packed_sums(dot_nt(beside(dab0), layers_beside(su0)), 0, True)
    for n in range(8):
        pack[n] = sums[8 * n : 8 * n + 8]

    first = []
    for s in far_first:
        to, peer = in_group(s)
        copy = pltpu.make_async_remote_copy(
            src_ref=pack.at[to], dst_ref=red_g.at[me_g],
            send_sem=red_send.at[0, s], recv_sem=red_recv.at[0, s],
            device_id=peer, device_id_type=MESH,
        )
        copy.start()
        first.append(copy)
    red_g[me_g] = pack[me_g]

    pbuf[0] = jnp.zeros_like(pbuf[0])
    pbuf[1] = jnp.zeros_like(pbuf[1])
    pbuf[10] = jnp.zeros_like(pbuf[0])
    pbuf[11] = jnp.zeros_like(pbuf[0])

    @pl.loop(0, 4, unroll=2)
    def _(p):
        q = dot(t3a[...], dab0[p])
        pbuf[2 * p + 2] = q[:, 0:128]
        pbuf[2 * p + 3] = q[:, 128:256]

    for n in range(10):
        part[n] = gather_sum(pbuf, n, -1)
    ring_x[0] = part[0, 8:16, :]
    ring_x[1] = part[9, 8:16, :]
    for side, row in ((0, 7), (1, 16)):
        ring_y[side] = jnp.concatenate([part[n, row : row + 1, :] for n in range(1, 9)], axis=0)
        for end, n in ((0, 0), (1, 9)):
            ring_c[end, side] = jnp.broadcast_to(part[n, row : row + 1, :], (8, 128))

    around = []
    for n, (dx, dy) in enumerate(sides):
        a, b = (0 if dx < 0 else 1), (0 if dy < 0 else 1)
        if dy == 0:
            src, dst = ring_x.at[a], back_x.at[a]
        elif dx == 0:
            src, dst = ring_y.at[b], back_y.at[b]
        else:
            src, dst = ring_c.at[a, b], back_c.at[a, b]
        copy = pltpu.make_async_remote_copy(
            src_ref=src, dst_ref=dst, send_sem=ring_send.at[n], recv_sem=ring_recv.at[n],
            device_id=near(dx, dy), device_id_type=MESH,
        )
        copy.start()
        around.append(copy)

    for copy in first:
        copy.wait()
    tile_y[...] = sum_slots(red_g)

    second = []
    for s in sorted(range(1, ny), key=lambda s: -min(s, ny - s)):
        copy = pltpu.make_async_remote_copy(
            src_ref=tile_y, dst_ref=red_y.at[py],
            send_sem=red_send.at[1, s], recv_sem=red_recv.at[1, s],
            device_id=along_y(s), device_id_type=MESH,
        )
        copy.start()
        second.append(copy)
    red_y[py] = tile_y[...]

    for copy in around:
        copy.wait()
    for x in range(8):
        i = x + XOFF
        back = part[x + 1, 8:16, :]
        add_lo = back_y[1, x : x + 1, :] * myl
        add_hi = back_y[0, x : x + 1, :] * myh
        if x == 0:
            back = back + back_x[1] * mxl
            add_lo = add_lo + back_c[1, 1, 0:1, :] * (mxl * myl)
            add_hi = add_hi + back_c[1, 0, 0:1, :] * (mxl * myh)
        if x == 7:
            back = back + back_x[0] * mxh
            add_lo = add_lo + back_c[0, 1, 0:1, :] * (mxh * myl)
            add_hi = add_hi + back_c[0, 0, 0:1, :] * (mxh * myh)
        back = back + jnp.where(row8 == 0, add_lo, 0.0) + jnp.where(row8 == 7, add_hi, 0.0)
        smooth = smooth_at(g1, w0, i)[8:16]
        out_grad[x] = g1[i, 8:16, :] - TAU * smooth + back + TAU * upstream[x]

    for copy in second:
        copy.wait()
    tile_z[...] = sum_slots(red_y)
    third = []
    for s in sorted(range(1, nz), key=lambda s: -min(s, nz - s)):
        copy = pltpu.make_async_remote_copy(
            src_ref=tile_z, dst_ref=red_z.at[pz],
            send_sem=red_send.at[2, s], recv_sem=red_recv.at[2, s],
            device_id=along_z(s), device_id_type=MESH,
        )
        copy.start()
        third.append(copy)
    red_z[pz] = tile_z[...]
    for copy in third:
        copy.wait()
    tile_f[...] = sum_slots(red_z)
    fourth = []
    for s in far_first:
        to, peer = in_group(s)
        copy = pltpu.make_async_remote_copy(
            src_ref=tile_f, dst_ref=final.at[me_g],
            send_sem=red_send.at[3, s], recv_sem=red_recv.at[3, s],
            device_id=peer, device_id_type=MESH,
        )
        copy.start()
        fourth.append(copy)
    final[me_g] = tile_f[...]
    for copy in fourth:
        copy.wait()

    scale = 1.0 / 2048.0
    whole = final[...].reshape(CH, 128) * scale
    turned = whole.T
    for k in range(2):
        out_w1[:, k, :] = turned[64 * k : 64 * k + 27, :]
        out_w2[:, k, :] = turned[64 * k + 32 : 64 * k + 59, :]
        out_b[k : k + 1, :] = turned[64 * k + 27 : 64 * k + 28, :]


def sum_slots(store):
    total = store[0]
    for n in range(1, store.shape[0]):
        total = total + store[n]
    return total


def hand_over(*refs):
    srcs, dsts, sems = refs[:4], refs[4:8], refs[8]
    copies = [pltpu.make_async_copy(s, d, sems.at[n]) for n, (s, d) in enumerate(zip(srcs, dsts))]
    for copy in copies:
        copy.start()
    for copy in copies:
        copy.wait()


def body(noisy, weights, filter_in, bias, filter_out, upstream):
    size_x, size_y = lax.axis_size("gx"), lax.axis_size("gy")
    field = pltpu.VMEM((LAYERS_X, ROWS, 128), F32)
    stack = pltpu.VMEM((LAYERS_X, SLAB, 128), BF16)
    vm = lambda *shape: pltpu.VMEM(shape, F32)
    vb = lambda *shape: pltpu.VMEM(shape, BF16)
    dma = lambda *shape: pltpu.SemaphoreType.DMA(shape)
    scratch = [
        vm(8, 8, 128), vm(2, 8, 8, 128), vb(27, 2, CH), vm(2, CH), vb(27, 2, CH), vm(8, 8, 128),
        vb(8, 32, 128), vb(8, 16, 128), vb(8, 16, 128), vb(2, 5, 32, 128), vb(2, LAYERS_X, 16, 128),
        field, field, field, field, field, field,
        stack, stack, stack, stack,
        vb(16 * CH, DEPTH), vb(12 * CH, DEPTH), vb(12 * CH, DEPTH), vb(8 * CH, DEPTH),
        vb(9 * GROWS, 16 * CH), vb(9 * GROWS, 12 * CH), vb(9 * GROWS, 8 * CH),
        vm(2, 32, CH), vm(2, 32, CH),
        vm(16, 9 * GROWS, 128), vm(12, 9 * GROWS, 128),
        vb(4, 8 * CH, 256), vm(4, 8 * CH, 256), vb(4, 8 * CH, 256), vb(4, 8 * CH, 256), vb(4, 8 * CH, 256),
        vm(2, 8, 128), vm(2, 8, 128), vm(2, 2, 8, 128), vm(2, 8, 128), vm(2, 8, 128), vm(2, 2, 8, 128), vm(10, ROWS, 128),
        vm(8, 8, 128), vm(8, 8, 128), vm(size_x // 4, 8, 128), vm(size_y // 2, 8, 128),
        vm(8, 128), vm(8, 128), vm(8, 128), vm(8, 8, 128),
        dma(6), dma(8), dma(8), dma(8), dma(8), dma(4, 8), dma(4, 8),
    ]
    spec = pl.BlockSpec(memory_space=pltpu.VMEM)
    far = pl.BlockSpec(memory_space=pltpu.HBM)
    shapes = (
        jax.ShapeDtypeStruct((8, 8, 128), F32),
        jax.ShapeDtypeStruct((27, 2, CH), F32),
        jax.ShapeDtypeStruct((27, 2, CH), F32),
        jax.ShapeDtypeStruct((2, CH), F32),
    )
    results = pl.pallas_call(
        functools.partial(kernel, size_x, size_y),
        out_shape=shapes,
        in_specs=[far] * 6,
        out_specs=(spec,) * 4,
        scratch_shapes=scratch,
        compiler_params=pltpu.CompilerParams(
            collective_id=0, has_side_effects=True, vmem_limit_bytes=60 * 1024 * 1024
        ),
    )(
        noisy, weights, jnp.transpose(filter_in, (2, 0, 1)), bias,
        jnp.transpose(filter_out, (1, 0, 2)), upstream,
    )
    grad, w1, w2, b = pl.pallas_call(
        hand_over,
        out_shape=shapes,
        in_specs=[far] * 4,
        out_specs=(far,) * 4,
        scratch_shapes=[pltpu.SemaphoreType.DMA((4,))],
        compiler_params=pltpu.CompilerParams(vmem_limit_bytes=60 * 1024 * 1024),
    )(*results)
    return grad, jnp.transpose(w1, (1, 2, 0)), jnp.transpose(w2, (1, 0, 2)), b


def solution(mesh):
    return jax.shard_map(
        body,
        mesh=mesh,
        in_specs=(
            P("gx", "gy", None),
            P(None, "gx", "gy", None),
            P(),
            P(),
            P(),
            P("gx", "gy", None),
        ),
        out_specs=(P("gx", "gy", None), P(), P(), P()),
        check_vma=False,
    )
```

```python
import functools

import jax
import jax.numpy as jnp
from jax import lax
from jax.experimental import pallas as pl
from jax.experimental.pallas import tpu as pltpu
from jax.sharding import PartitionSpec as P

TAU = 0.15
F32 = jnp.float32
BF16 = jnp.bfloat16
MESH = pl.DeviceIdType.MESH
CH = 64
ROWS = 24
XOFF = 5
LAYERS_X = 18
SLAB = 80
DEPTH = 3 * SLAB
GROWS = 16
GBASE = 4


def iota(shape, axis):
    return lax.broadcasted_iota(jnp.int32, shape, axis)


def move_z(v, step):
    lane = iota(v.shape, 1)
    if step == 1:
        return jnp.where(lane == 127, 0.0, pltpu.roll(v, 127, 1))
    return jnp.where(lane == 0, 0.0, pltpu.roll(v, 1, 1))


def move_y(v, step):
    return pltpu.roll(v, (-step) % v.shape[0], 0)


def slab_of(v):
    ones = jnp.ones((SLAB - 3 * ROWS, 128), F32)
    return jnp.concatenate([move_z(v, -1), v, move_z(v, 1), ones], axis=0).astype(BF16)


def flux_x(v, w, i):
    return w[i] * (v[i + 1] - v[i])


def smooth_at(v, w, i):
    here, factor = v[i], w[i]
    fy = factor * (move_y(here, 1) - here)
    fz = factor * (move_z(here, 1) - here)
    return (
        flux_x(v, w, i - 1) - flux_x(v, w, i) + (move_y(fy, -1) - fy) + (move_z(fz, -1) - fz)
    )


def split_column(shape, axis):
    k = iota(shape, axis)
    sx = (k >= SLAB).astype(jnp.int32) + (k >= 2 * SLAB).astype(jnp.int32)
    rest = k - SLAB * sx
    sz = (rest >= ROWS).astype(jnp.int32) + (rest >= 2 * ROWS).astype(jnp.int32)
    row = rest - ROWS * sz
    good = (rest < 3 * ROWS) & (k < DEPTH)
    return sx, sz, row, good, rest


def split_rows(shape, axis):
    m = iota(shape, axis)
    s = sum((m >= GROWS * n).astype(jnp.int32) for n in range(1, 9))
    row = m - GROWS * s + GBASE
    sx = (s >= 3).astype(jnp.int32) + (s >= 6).astype(jnp.int32)
    return sx, s - 3 * sx, row


def one_hot(hit):
    return jnp.where(hit, 1.0, 0.0).astype(BF16)


def dot(a, b):
    return jnp.dot(a, b, preferred_element_type=F32)


def dot_nt(a, b):
    return lax.dot_general(a, b, (((1,), (1,)), ((), ())), preferred_element_type=F32)


def thirds(v):
    high = v.astype(BF16)
    rest = v - high.astype(F32)
    mid = rest.astype(BF16)
    low = (rest - mid.astype(F32)).astype(BF16)
    return high, mid, low


def fill_patch(out, weight, bias_col, ys):
    shape = (32, DEPTH)
    sx, sz, row, good, _ = split_column(shape, 1)
    base = 9 * sx + sz
    j = iota(shape, 0)
    k = iota((CH, DEPTH), 1)
    extra = jnp.zeros((CH, DEPTH), F32)
    for n, part in enumerate(thirds(bias_col)):
        extra = extra + jnp.where(k == SLAB + 3 * ROWS + n, part.astype(F32), 0.0)
    for n, y in enumerate(ys):
        step = row - (y + 7)
        hit = good & (step >= 0) & (step <= 2) & (j == base + 3 * step)
        block = (dot(weight, one_hot(hit)) + extra) * 0.5
        out[n * CH : (n + 1) * CH, :] = block.astype(BF16)


def fill_spread(out, weight_t, ys):
    shape = (32, DEPTH)
    sx, sz, row, good, _ = split_column(shape, 1)
    base = 9 * (2 - sx) + (2 - sz)
    j = iota(shape, 0)
    for n, y in enumerate(ys):
        step = (y + 9) - row
        hit = good & (step >= 0) & (step <= 2) & (j == base + 3 * step)
        out[n * CH : (n + 1) * CH, :] = (dot(weight_t, one_hot(hit)) * 0.5).astype(BF16)


def fill_gather(out, weight, ys, sign, low, high):
    shape = (9 * GROWS, 32)
    sx, sz, row = split_rows(shape, 0)
    base = 9 * sx + sz
    j = iota(shape, 1)
    for n in range(0, len(ys), 2):
        halves = []
        for y in ys[n : n + 2]:
            step = (y + 9) - row if sign > 0 else row - (y + 7)
            hit = (step >= 0) & (step <= 2) & (j == base + 3 * step)
            part = one_hot(hit)
            half = dot(part, weight)
            if y < 0:
                half = half * low
            elif y > 7:
                half = half * high
            halves.append(half)
        out[:, n * CH : (n + 2) * CH] = jnp.concatenate(halves, axis=1).astype(BF16)


def pair_of(stack, i):
    left = stack[pl.ds(i - 1, 3)].reshape(DEPTH, 128)
    right = stack[pl.ds(i, 3)].reshape(DEPTH, 128)
    return jnp.concatenate([left, right], axis=1)


def gather_sum(store, n, sign):
    total = None
    for sz in range(3):
        part = None
        for sx in range(3):
            at = n + sx if sign > 0 else n + 2 - sx
            lo = (3 * sx + sz) * GROWS
            term = store[at, lo : lo + GROWS, :]
            part = term if part is None else part + term
        if sz != 1:
            part = move_z(part, sign * (sz - 1))
        total = part if total is None else total + part
    pad = jnp.zeros((GBASE, 128), F32)
    return jnp.concatenate([pad, total, pad], axis=0)


def fold_rows(out):
    total = out[0:CH]
    for y in range(1, 8):
        total = total + pltpu.roll(out[y * CH : (y + 1) * CH], 256 - y, 1)
    return total


def pick_columns(layer, first):
    shape = (256, 128)
    sx, sz, row, good, rest = split_column(shape, 0)
    lane = iota(shape, 1)
    if first:
        step = row - 7
        j = 9 * sx + 3 * step + sz
        ok = good & (step >= 0) & (step <= 2)
        hit = ok & (lane == 64 * layer + j)
        spare = (sx == 1) & (rest == 3 * ROWS) & (lane == 64 * layer + 27)
        return one_hot(hit | spare)
    step = 9 - row
    j = 9 * (2 - sx) + 3 * step + (2 - sz)
    ok = good & (step >= 0) & (step <= 2)
    return one_hot(ok & (lane == 64 * layer + 32 + j))


def packed_sums(out, layer, first):
    folded = fold_rows(out)
    pick = pick_columns(layer, first)
    high, mid, low = thirds(folded)
    return dot(high, pick) + dot(mid, pick) + dot(low, pick)


def layers_beside(stack):
    parts = [stack[i - 1 : i + 2].reshape(DEPTH, 128) for i in range(XOFF, XOFF + 8)]
    whole = jnp.concatenate(parts, axis=1)
    return jnp.concatenate([whole, jnp.zeros((256 - DEPTH, 1024), BF16)], axis=0)


def kernel(
    size_x, size_y,
    noisy_at, weights_at, filter_in_at, bias_at, filter_out_at, upstream_at,
    out_grad, out_w1, out_w2, out_b,
    noisy, weights, filter_in, bias, filter_out, upstream,
    send_x, send_yl, send_yh, got_x, got_y,
    u0, g0, w0, w1, u1, g1,
    su0, ss1, su1, ss0,
    t1a, t1b, t2b, t2a, toa, t3b, t3a,
    pad_in, pad_out,
    qbuf, pbuf, h0, d0, h1, dab1, dab0,
    ring_x, ring_y, ring_c, back_x, back_y, back_c, part,
    pack, red_g, red_y, red_z, tile_y, tile_z, tile_f, final,
    fetch_sem, halo_send, halo_recv, ring_send, ring_recv, red_send, red_recv,
):
    gx, gy = lax.axis_index("gx"), lax.axis_index("gy")
    core, xlo, py = lax.rem(gx, 2), lax.rem(gx // 2, 2), gx // 4
    xhi, pz = lax.rem(gy, 2), gy // 2
    ny, nz = size_x // 4, size_y // 2
    me_g = (xhi * 2 + xlo) * 2 + core

    def near(dx, dy):
        return (lax.rem(gx + dx + size_x, size_x), lax.rem(gy + dy + size_y, size_y))

    def in_group(step):
        to = lax.rem(me_g + step, 8)
        c, x = lax.rem(to, 2), to // 2
        return to, (py * 4 + lax.rem(x, 2) * 2 + c, pz * 2 + x // 2)

    def along_y(step):
        return (lax.rem(py + step, ny) * 4 + xlo * 2 + core, gy)

    def along_z(step):
        return (gx, lax.rem(pz + step, nz) * 2 + xhi)

    sides = [(-1, -1), (1, 1), (-1, 1), (1, -1), (0, -1), (0, 1), (-1, 0), (1, 0)]
    far_first = (4, 3, 5, 2, 6, 1, 7)
    barrier = pltpu.get_barrier_semaphore()
    peers = [near(*side) for side in sides] + [in_group(s)[1] for s in range(1, 8)]
    peers += [along_y(s) for s in range(1, ny)] + [along_z(s) for s in range(1, nz)]
    for peer in peers:
        pl.semaphore_signal(barrier, inc=1, device_id=peer, device_id_type=MESH)

    fetched = [
        pltpu.make_async_copy(src, dst, fetch_sem.at[n])
        for n, (src, dst) in enumerate((
            (noisy_at, noisy), (upstream_at, upstream), (weights_at, weights),
            (filter_in_at, filter_in), (filter_out_at, filter_out), (bias_at, bias),
        ))
    ]
    for copy in fetched:
        copy.start()

    mxl = jnp.where(gx > 0, 1.0, 0.0).astype(F32)
    mxh = jnp.where(gx < size_x - 1, 1.0, 0.0).astype(F32)
    myl = jnp.where(gy > 0, 1.0, 0.0).astype(F32)
    myh = jnp.where(gy < size_y - 1, 1.0, 0.0).astype(F32)

    row8 = iota((8, 128), 0)
    for copy in fetched[:3]:
        copy.wait()
    for x in range(8):
        u, g, wa, wb = noisy[x], upstream[x], weights[0, x], weights[1, x]
        send_x[x] = jnp.concatenate([u, g, wa, wb], axis=0).astype(BF16)
        top = jnp.where(row8 < 5, pltpu.roll(u, 5, 0), g)
        low = jnp.where(row8 < 4, pltpu.roll(wa, 4, 0), pltpu.roll(wb, 6, 0))
        send_yl[x] = jnp.concatenate([top, low], axis=0).astype(BF16)
        top = jnp.where(row8 < 5, u, pltpu.roll(g, 5, 0))
        low = jnp.where(row8 < 4, wa, pltpu.roll(wb, 4, 0))
        send_yh[x] = jnp.concatenate([top, low], axis=0).astype(BF16)
    pl.semaphore_wait(barrier, len(peers))

    halo = []
    span = {-1: (0, 13), 0: (0, 5), 1: (3, 0)}
    for n, (dx, dy) in enumerate(sides):
        start, land = span[dx]
        if dy == 0:
            src, dst = send_x.at[pl.ds(start, 5)], got_x.at[0 if dx > 0 else 1]
        else:
            count = 8 if dx == 0 else 5
            src = (send_yl if dy > 0 else send_yh).at[pl.ds(start, count)]
            dst = got_y.at[0 if dy > 0 else 1, pl.ds(land, count)]
        copy = pltpu.make_async_remote_copy(
            src_ref=src, dst_ref=dst, send_sem=halo_send.at[n], recv_sem=halo_recv.at[n],
            device_id=near(dx, dy), device_id_type=MESH,
        )
        copy.start()
        halo.append(copy)

    eye = iota((CH, CH), 0) == iota((CH, CH), 1)
    for copy in fetched[3:]:
        copy.wait()
    pad_in[...] = jnp.zeros_like(pad_in)
    pad_out[...] = jnp.zeros_like(pad_out)
    whole_in, whole_out = filter_in[...].astype(F32), filter_out[...].astype(F32)
    cols = []
    for k in range(2):
        pad_in[k, 0:27, :] = whole_in[:, k, :]
        pad_out[k, 0:27, :] = whole_out[:, k, :]
        spread = jnp.broadcast_to(bias[k : k + 1, :], (CH, CH))
        cols.append(jnp.sum(jnp.where(eye, spread, 0.0), axis=1, keepdims=True))
    win_t = [pad_in[k].astype(BF16) for k in range(2)]
    wout = [pad_out[k].astype(BF16) for k in range(2)]
    win = [dot_nt(one_hot(eye), win_t[k]).astype(BF16) for k in range(2)]
    wout_t = [dot_nt(one_hot(eye), wout[k]).astype(BF16) for k in range(2)]
    fill_patch(t1a, win[0], cols[0], range(-4, 12))
    fill_gather(toa, wout[0], range(-4, 12), 1, myl, myh)
    fill_patch(t1b, win[1], cols[1], range(-2, 10))
    fill_spread(t2b, wout_t[1], range(-2, 10))
    fill_gather(t3b, win_t[1], range(-2, 10), -1, myl, myh)
    fill_spread(t2a, wout_t[0], range(0, 8))
    fill_gather(t3a, win_t[0], range(0, 8), -1, myl, myh)

    for copy in halo:
        copy.wait()

    for i in range(LAYERS_X):
        if i < XOFF:
            rows, edge = got_x[0, i].astype(F32) * mxl, mxl
        elif i >= XOFF + 8:
            rows, edge = got_x[1, i - XOFF - 8].astype(F32) * mxh, mxh
        else:
            x, edge = i - XOFF, jnp.float32(1.0)
            rows = jnp.concatenate([noisy[x], upstream[x], weights[0, x], weights[1, x]], axis=0)
        lo = got_y[0, i].astype(F32) * (edge * myl)
        hi = got_y[1, i].astype(F32) * (edge * myh)
        lo_t, lo_b, hi_t, hi_b = lo[0:8], lo[8:16], hi[0:8], hi[8:16]
        u = jnp.concatenate([pltpu.roll(lo_t, 3, 0), rows[0:8], hi_t], axis=0)
        u0[i] = u
        su0[i] = slab_of(u)
        w0[i] = jnp.concatenate([pltpu.roll(lo_b, 4, 0), rows[16:24], hi_b], axis=0)
        if 2 <= i < 16:
            g = jnp.concatenate([lo_t, rows[8:16], pltpu.roll(hi_t, 3, 0)], axis=0)
            g0[i] = g
            ss1[i] = slab_of(-TAU * g)
            w1[i] = jnp.concatenate(
                [pltpu.roll(lo_b, 2, 0), rows[24:32], pltpu.roll(hi_b, 4, 0)], axis=0
            )

    row24 = iota((ROWS, 128), 0)
    inside_y = jnp.where(row24 < 8, myl, jnp.where(row24 < 16, 1.0, myh))

    def x_mask(i):
        return jnp.where(i < XOFF, mxl, jnp.where(i >= XOFF + 8, mxh, 1.0))

    def forward(p, keep):
        slot = jnp.where(p < 6, p - 2, 4)
        i = 1 + 2 * p
        rhs = pair_of(su0, i)
        q = None
        for m in range(4):
            cut = slice(4 * CH * m, 4 * CH * (m + 1))
            half = dot(t1a[cut, :], rhs)
            t = jnp.tanh(half)
            h = half + half * t
            hb = h.astype(BF16)
            if keep and m in (1, 2):
                own = slice(4 * CH * (m - 1), 4 * CH * m)
                h0[slot, own, :] = hb
                d0[slot, own, :] = (1.0 + t) + (h - h * t)
            term = dot(toa[:, cut], hb)
            q = term if q is None else q + term
        qbuf[2 * p] = q[:, 0:128] * x_mask(i)
        qbuf[2 * p + 1] = q[:, 128:256] * x_mask(i + 1)

    def iterate(n):
        i = n + 2
        learned = gather_sum(qbuf, n, 1)
        v = u0[i] - TAU * (smooth_at(u0, w0, i) + learned)
        su1[i] = slab_of(v * (inside_y * x_mask(i)))

    @pl.loop(0, 2, unroll=2)
    def _(p):
        forward(p, False)

    @pl.loop(2, 8, unroll=2)
    def _(p):
        iterate(2 * p - 4)
        iterate(2 * p - 3)
        forward(p, True)

    iterate(12)
    iterate(13)

    def middle(p, slot):
        i = 3 + 2 * p
        rhs_u, rhs_s = pair_of(su1, i), pair_of(ss1, i)
        q = None
        for first, last in ((0, 2), (2, 6), (6, 10), (10, 12)):
            cut = slice(CH * first, CH * last)
            half = dot(t1b[cut, :], rhs_u)
            dh = dot(t2b[cut, :], rhs_s)
            t = jnp.tanh(half)
            h = half + half * t
            dab = (dh * ((1.0 + t) + (h - h * t))).astype(BF16)
            if last - first == 4:
                own = slice(CH * (first - 2), CH * (last - 2))
                h1[slot, own, :] = h.astype(BF16)
                dab1[slot, own, :] = dab
            term = dot(t3b[:, cut], dab)
            q = term if q is None else q + term
        pbuf[2 * p] = q[:, 0:128] * x_mask(i)
        pbuf[2 * p + 1] = q[:, 128:256] * x_mask(i + 1)

    def cotangent(n):
        i = n + 4
        g = g0[i]
        v = g - TAU * (g + smooth_at(g0, w1, i)) + gather_sum(pbuf, n, -1)
        v = v * (inside_y * x_mask(i))
        g1[i] = v
        ss0[i] = slab_of(-TAU * v)

    @pl.loop(0, 2, unroll=2)
    def _(p):
        middle(p, jnp.where(p > 0, 0, 4))

    @pl.loop(2, 6, unroll=2)
    def _(p):
        cotangent(2 * p - 4)
        cotangent(2 * p - 3)
        middle(p, jnp.where(p < 5, p - 1, 4))

    cotangent(8)
    cotangent(9)

    def beside(store):
        return jnp.concatenate([store[p] for p in range(4)], axis=1)

    sums = packed_sums(dot_nt(beside(h1), layers_beside(ss1)), 1, False)
    sums = sums + packed_sums(dot_nt(beside(dab1), layers_beside(su1)), 1, True)

    @pl.loop(0, 4, unroll=4)
    def _(p):
        dh = dot(t2a[...], pair_of(ss0, XOFF + 2 * p))
        dab0[p] = (dh * d0[p]).astype(BF16)

    sums = sums + packed_sums(dot_nt(beside(h0), layers_beside(ss0)), 0, False)
    sums = sums + packed_sums(dot_nt(beside(dab0), layers_beside(su0)), 0, True)
    for n in range(8):
        pack[n] = sums[8 * n : 8 * n + 8]

    first = []
    for s in far_first:
        to, peer = in_group(s)
        copy = pltpu.make_async_remote_copy(
            src_ref=pack.at[to], dst_ref=red_g.at[me_g],
            send_sem=red_send.at[0, s], recv_sem=red_recv.at[0, s],
            device_id=peer, device_id_type=MESH,
        )
        copy.start()
        first.append(copy)
    red_g[me_g] = pack[me_g]

    pbuf[0] = jnp.zeros_like(pbuf[0])
    pbuf[1] = jnp.zeros_like(pbuf[1])
    pbuf[10] = jnp.zeros_like(pbuf[0])
    pbuf[11] = jnp.zeros_like(pbuf[0])

    @pl.loop(0, 4, unroll=2)
    def _(p):
        q = dot(t3a[...], dab0[p])
        pbuf[2 * p + 2] = q[:, 0:128]
        pbuf[2 * p + 3] = q[:, 128:256]

    for n in range(10):
        part[n] = gather_sum(pbuf, n, -1)
    ring_x[0] = part[0, 8:16, :]
    ring_x[1] = part[9, 8:16, :]
    for side, row in ((0, 7), (1, 16)):
        ring_y[side] = jnp.concatenate([part[n, row : row + 1, :] for n in range(1, 9)], axis=0)
        for end, n in ((0, 0), (1, 9)):
            ring_c[end, side] = jnp.broadcast_to(part[n, row : row + 1, :], (8, 128))

    around = []
    for n, (dx, dy) in enumerate(sides):
        a, b = (0 if dx < 0 else 1), (0 if dy < 0 else 1)
        if dy == 0:
            src, dst = ring_x.at[a], back_x.at[a]
        elif dx == 0:
            src, dst = ring_y.at[b], back_y.at[b]
        else:
            src, dst = ring_c.at[a, b], back_c.at[a, b]
        copy = pltpu.make_async_remote_copy(
            src_ref=src, dst_ref=dst, send_sem=ring_send.at[n], recv_sem=ring_recv.at[n],
            device_id=near(dx, dy), device_id_type=MESH,
        )
        copy.start()
        around.append(copy)

    for copy in first:
        copy.wait()
    tile_y[...] = sum_slots(red_g)

    second = []
    for s in sorted(range(1, ny), key=lambda s: -min(s, ny - s)):
        copy = pltpu.make_async_remote_copy(
            src_ref=tile_y, dst_ref=red_y.at[py],
            send_sem=red_send.at[1, s], recv_sem=red_recv.at[1, s],
            device_id=along_y(s), device_id_type=MESH,
        )
        copy.start()
        second.append(copy)
    red_y[py] = tile_y[...]

    for copy in around:
        copy.wait()
    for x in range(8):
        i = x + XOFF
        back = part[x + 1, 8:16, :]
        add_lo = back_y[1, x : x + 1, :] * myl
        add_hi = back_y[0, x : x + 1, :] * myh
        if x == 0:
            back = back + back_x[1] * mxl
            add_lo = add_lo + back_c[1, 1, 0:1, :] * (mxl * myl)
            add_hi = add_hi + back_c[1, 0, 0:1, :] * (mxl * myh)
        if x == 7:
            back = back + back_x[0] * mxh
            add_lo = add_lo + back_c[0, 1, 0:1, :] * (mxh * myl)
            add_hi = add_hi + back_c[0, 0, 0:1, :] * (mxh * myh)
        back = back + jnp.where(row8 == 0, add_lo, 0.0) + jnp.where(row8 == 7, add_hi, 0.0)
        smooth = smooth_at(g1, w0, i)[8:16]
        out_grad[x] = g1[i, 8:16, :] - TAU * smooth + back + TAU * upstream[x]

    for copy in second:
        copy.wait()
    tile_z[...] = sum_slots(red_y)
    third = []
    for s in sorted(range(1, nz), key=lambda s: -min(s, nz - s)):
        copy = pltpu.make_async_remote_copy(
            src_ref=tile_z, dst_ref=red_z.at[pz],
            send_sem=red_send.at[2, s], recv_sem=red_recv.at[2, s],
            device_id=along_z(s), device_id_type=MESH,
        )
        copy.start()
        third.append(copy)
    red_z[pz] = tile_z[...]
    for copy in third:
        copy.wait()
    tile_f[...] = sum_slots(red_z)
    fourth = []
    for s in far_first:
        to, peer = in_group(s)
        copy = pltpu.make_async_remote_copy(
            src_ref=tile_f, dst_ref=final.at[me_g],
            send_sem=red_send.at[3, s], recv_sem=red_recv.at[3, s],
            device_id=peer, device_id_type=MESH,
        )
        copy.start()
        fourth.append(copy)
    final[me_g] = tile_f[...]
    for copy in fourth:
        copy.wait()

    scale = 1.0 / 2048.0
    whole = final[...].reshape(CH, 128) * scale
    turned = whole.T
    for k in range(2):
        out_w1[:, k, :] = turned[64 * k : 64 * k + 27, :]
        out_w2[:, k, :] = turned[64 * k + 32 : 64 * k + 59, :]
        out_b[k : k + 1, :] = turned[64 * k + 27 : 64 * k + 28, :]


def sum_slots(store):
    total = store[0]
    for n in range(1, store.shape[0]):
        total = total + store[n]
    return total


def body(noisy, weights, filter_in, bias, filter_out, upstream):
    size_x, size_y = lax.axis_size("gx"), lax.axis_size("gy")
    field = pltpu.VMEM((LAYERS_X, ROWS, 128), F32)
    stack = pltpu.VMEM((LAYERS_X, SLAB, 128), BF16)
    vm = lambda *shape: pltpu.VMEM(shape, F32)
    vb = lambda *shape: pltpu.VMEM(shape, BF16)
    dma = lambda *shape: pltpu.SemaphoreType.DMA(shape)
    scratch = [
        vm(8, 8, 128), vm(2, 8, 8, 128), vb(27, 2, CH), vm(2, CH), vb(27, 2, CH), vm(8, 8, 128),
        vb(8, 32, 128), vb(8, 16, 128), vb(8, 16, 128), vb(2, 5, 32, 128), vb(2, LAYERS_X, 16, 128),
        field, field, field, field, field, field,
        stack, stack, stack, stack,
        vb(16 * CH, DEPTH), vb(12 * CH, DEPTH), vb(12 * CH, DEPTH), vb(8 * CH, DEPTH),
        vb(9 * GROWS, 16 * CH), vb(9 * GROWS, 12 * CH), vb(9 * GROWS, 8 * CH),
        vm(2, 32, CH), vm(2, 32, CH),
        vm(16, 9 * GROWS, 128), vm(12, 9 * GROWS, 128),
        vb(5, 8 * CH, 256), vm(5, 8 * CH, 256), vb(5, 8 * CH, 256), vb(5, 8 * CH, 256), vb(4, 8 * CH, 256),
        vm(2, 8, 128), vm(2, 8, 128), vm(2, 2, 8, 128), vm(2, 8, 128), vm(2, 8, 128), vm(2, 2, 8, 128), vm(10, ROWS, 128),
        vm(8, 8, 128), vm(8, 8, 128), vm(size_x // 4, 8, 128), vm(size_y // 2, 8, 128),
        vm(8, 128), vm(8, 128), vm(8, 128), vm(8, 8, 128),
        dma(6), dma(8), dma(8), dma(8), dma(8), dma(4, 8), dma(4, 8),
    ]
    spec = pl.BlockSpec(memory_space=pltpu.VMEM)
    far = pl.BlockSpec(memory_space=pltpu.HBM)
    shapes = (vm(8, 8, 128), vm(27, 2, CH), vm(27, 2, CH), vm(2, CH))
    grad, w1, w2, b = pl.pallas_call(
        functools.partial(kernel, size_x, size_y),
        out_shape=shapes,
        in_specs=[far] * 6,
        out_specs=(spec,) * 4,
        scratch_shapes=scratch,
        compiler_params=pltpu.CompilerParams(
            collective_id=0, has_side_effects=True, vmem_limit_bytes=60 * 1024 * 1024
        ),
    )(
        noisy, weights, jnp.transpose(filter_in, (2, 0, 1)), bias,
        jnp.transpose(filter_out, (1, 0, 2)), upstream,
    )
    return grad, jnp.transpose(w1, (1, 2, 0)), jnp.transpose(w2, (1, 0, 2)), b


def solution(mesh):
    return jax.shard_map(
        body,
        mesh=mesh,
        in_specs=(
            P("gx", "gy", None),
            P(None, "gx", "gy", None),
            P(),
            P(),
            P(),
            P("gx", "gy", None),
        ),
        out_specs=(P("gx", "gy", None), P(), P(), P()),
        check_vma=False,
    )
```

```python
import functools

import jax
import jax.numpy as jnp
from jax import lax
from jax.experimental import pallas as pl
from jax.experimental.pallas import tpu as pltpu
from jax.sharding import PartitionSpec as P

TAU = 0.15
F32 = jnp.float32
BF16 = jnp.bfloat16
MESH = pl.DeviceIdType.MESH
CH = 64
ROWS = 24
XOFF = 5
LAYERS_X = 18
SLAB = 80
DEPTH = 3 * SLAB
GROWS = 16
GBASE = 4


def iota(shape, axis):
    return lax.broadcasted_iota(jnp.int32, shape, axis)


def move_z(v, step):
    lane = iota(v.shape, 1)
    if step == 1:
        return jnp.where(lane == 127, 0.0, pltpu.roll(v, 127, 1))
    return jnp.where(lane == 0, 0.0, pltpu.roll(v, 1, 1))


def move_y(v, step):
    return pltpu.roll(v, (-step) % v.shape[0], 0)


def slab_of(v):
    ones = jnp.ones((SLAB - 3 * ROWS, 128), F32)
    return jnp.concatenate([move_z(v, -1), v, move_z(v, 1), ones], axis=0).astype(BF16)


def flux_x(v, w, i):
    return w[i] * (v[i + 1] - v[i])


def smooth_at(v, w, i):
    here, factor = v[i], w[i]
    fy = factor * (move_y(here, 1) - here)
    fz = factor * (move_z(here, 1) - here)
    return (
        flux_x(v, w, i - 1) - flux_x(v, w, i) + (move_y(fy, -1) - fy) + (move_z(fz, -1) - fz)
    )


def split_column(shape, axis):
    k = iota(shape, axis)
    sx = (k >= SLAB).astype(jnp.int32) + (k >= 2 * SLAB).astype(jnp.int32)
    rest = k - SLAB * sx
    sz = (rest >= ROWS).astype(jnp.int32) + (rest >= 2 * ROWS).astype(jnp.int32)
    row = rest - ROWS * sz
    good = (rest < 3 * ROWS) & (k < DEPTH)
    return sx, sz, row, good, rest


def split_rows(shape, axis):
    m = iota(shape, axis)
    s = sum((m >= GROWS * n).astype(jnp.int32) for n in range(1, 9))
    row = m - GROWS * s + GBASE
    sx = (s >= 3).astype(jnp.int32) + (s >= 6).astype(jnp.int32)
    return sx, s - 3 * sx, row


def one_hot(hit):
    return jnp.where(hit, 1.0, 0.0).astype(BF16)


def dot(a, b):
    return jnp.dot(a, b, preferred_element_type=F32)


def dot_nt(a, b):
    return lax.dot_general(a, b, (((1,), (1,)), ((), ())), preferred_element_type=F32)


def thirds(v):
    high = v.astype(BF16)
    rest = v - high.astype(F32)
    mid = rest.astype(BF16)
    low = (rest - mid.astype(F32)).astype(BF16)
    return high, mid, low


def fill_patch(out, weight, bias_col, ys):
    shape = (32, DEPTH)
    sx, sz, row, good, _ = split_column(shape, 1)
    base = 9 * sx + sz
    j = iota(shape, 0)
    k = iota((CH, DEPTH), 1)
    extra = jnp.zeros((CH, DEPTH), F32)
    for n, part in enumerate(thirds(bias_col)):
        extra = extra + jnp.where(k == SLAB + 3 * ROWS + n, part.astype(F32), 0.0)
    for n, y in enumerate(ys):
        step = row - (y + 7)
        hit = good & (step >= 0) & (step <= 2) & (j == base + 3 * step)
        block = (dot(weight, one_hot(hit)) + extra) * 0.5
        out[n * CH : (n + 1) * CH, :] = block.astype(BF16)


def fill_spread(out, weight_t, ys):
    shape = (32, DEPTH)
    sx, sz, row, good, _ = split_column(shape, 1)
    base = 9 * (2 - sx) + (2 - sz)
    j = iota(shape, 0)
    for n, y in enumerate(ys):
        step = (y + 9) - row
        hit = good & (step >= 0) & (step <= 2) & (j == base + 3 * step)
        out[n * CH : (n + 1) * CH, :] = (dot(weight_t, one_hot(hit)) * 0.5).astype(BF16)


def fill_gather(out, weight, ys, sign, low, high):
    shape = (9 * GROWS, 32)
    sx, sz, row = split_rows(shape, 0)
    base = 9 * sx + sz
    j = iota(shape, 1)
    for n in range(0, len(ys), 2):
        halves = []
        for y in ys[n : n + 2]:
            step = (y + 9) - row if sign > 0 else row - (y + 7)
            hit = (step >= 0) & (step <= 2) & (j == base + 3 * step)
            part = one_hot(hit)
            half = dot(part, weight)
            if y < 0:
                half = half * low
            elif y > 7:
                half = half * high
            halves.append(half)
        out[:, n * CH : (n + 2) * CH] = jnp.concatenate(halves, axis=1).astype(BF16)


def pair_of(stack, i):
    left = stack[pl.ds(i - 1, 3)].reshape(DEPTH, 128)
    right = stack[pl.ds(i, 3)].reshape(DEPTH, 128)
    return jnp.concatenate([left, right], axis=1)


def gather_sum(store, n, sign):
    total = None
    for sz in range(3):
        part = None
        for sx in range(3):
            at = n + sx if sign > 0 else n + 2 - sx
            lo = (3 * sx + sz) * GROWS
            term = store[at, lo : lo + GROWS, :]
            part = term if part is None else part + term
        if sz != 1:
            part = move_z(part, sign * (sz - 1))
        total = part if total is None else total + part
    pad = jnp.zeros((GBASE, 128), F32)
    return jnp.concatenate([pad, total, pad], axis=0)


def fold_rows(out):
    total = out[0:CH]
    for y in range(1, 8):
        total = total + pltpu.roll(out[y * CH : (y + 1) * CH], 256 - y, 1)
    return total


def pick_columns(layer, first):
    shape = (256, 128)
    sx, sz, row, good, rest = split_column(shape, 0)
    lane = iota(shape, 1)
    if first:
        step = row - 7
        j = 9 * sx + 3 * step + sz
        ok = good & (step >= 0) & (step <= 2)
        hit = ok & (lane == 64 * layer + j)
        spare = (sx == 1) & (rest == 3 * ROWS) & (lane == 64 * layer + 27)
        return one_hot(hit | spare)
    step = 9 - row
    j = 9 * (2 - sx) + 3 * step + (2 - sz)
    ok = good & (step >= 0) & (step <= 2)
    return one_hot(ok & (lane == 64 * layer + 32 + j))


def packed_sums(out, pick):
    folded = fold_rows(out)
    high, mid, low = thirds(folded)
    return dot(high, pick) + dot(mid, pick) + dot(low, pick)


def layers_beside(stack):
    parts = [stack[i - 1 : i + 2].reshape(DEPTH, 128) for i in range(XOFF, XOFF + 8)]
    whole = jnp.concatenate(parts, axis=1)
    return jnp.concatenate([whole, jnp.zeros((256 - DEPTH, 1024), BF16)], axis=0)


def kernel(
    size_x, size_y,
    noisy_at, weights_at, filter_in_at, bias_at, filter_out_at, upstream_at,
    out_grad, out_p,
    noisy, weights, filter_in, bias, filter_out, upstream,
    send_x, send_yl, send_yh, got_x, got_y,
    u0, g0, w0, w1, u1, g1,
    su0, ss1, su1, ss0,
    t1a, t1b, t2b, t2a, toa, t3b, t3a,
    pad_in, pad_out, picks,
    qbuf, pbuf, h0, d0, h1, dab1, dab0,
    ring_x, ring_y, ring_c, back_x, back_y, back_c, part,
    pack, red_g, red_y, red_z, tile_y, tile_z, tile_f, final,
    fetch_sem, halo_send, halo_recv, ring_send, ring_recv, red_send, red_recv,
):
    gx, gy = lax.axis_index("gx"), lax.axis_index("gy")
    core, xlo, py = lax.rem(gx, 2), lax.rem(gx // 2, 2), gx // 4
    xhi, pz = lax.rem(gy, 2), gy // 2
    ny, nz = size_x // 4, size_y // 2
    me_g = (xhi * 2 + xlo) * 2 + core

    def near(dx, dy):
        return (lax.rem(gx + dx + size_x, size_x), lax.rem(gy + dy + size_y, size_y))

    def in_group(step):
        to = lax.rem(me_g + step, 8)
        c, x = lax.rem(to, 2), to // 2
        return to, (py * 4 + lax.rem(x, 2) * 2 + c, pz * 2 + x // 2)

    def along_y(step):
        return (lax.rem(py + step, ny) * 4 + xlo * 2 + core, gy)

    def along_z(step):
        return (gx, lax.rem(pz + step, nz) * 2 + xhi)

    sides = [(-1, -1), (1, 1), (-1, 1), (1, -1), (0, -1), (0, 1), (-1, 0), (1, 0)]
    far_first = (4, 3, 5, 2, 6, 1, 7)
    barrier = pltpu.get_barrier_semaphore()
    peers = [near(*side) for side in sides] + [in_group(s)[1] for s in range(1, 8)]
    peers += [along_y(s) for s in range(1, ny)] + [along_z(s) for s in range(1, nz)]
    for peer in peers[: len(sides)]:
        pl.semaphore_signal(barrier, inc=1, device_id=peer, device_id_type=MESH)
    fetched = [
        pltpu.make_async_copy(src, dst, fetch_sem.at[n])
        for n, (src, dst) in enumerate((
            (noisy_at, noisy), (upstream_at, upstream), (weights_at, weights),
            (filter_in_at, filter_in), (filter_out_at, filter_out), (bias_at, bias),
        ))
    ]
    for copy in fetched:
        copy.start()
    for peer in peers[len(sides) :]:
        pl.semaphore_signal(barrier, inc=1, device_id=peer, device_id_type=MESH)

    mxl = jnp.where(gx > 0, 1.0, 0.0).astype(F32)
    mxh = jnp.where(gx < size_x - 1, 1.0, 0.0).astype(F32)
    myl = jnp.where(gy > 0, 1.0, 0.0).astype(F32)
    myh = jnp.where(gy < size_y - 1, 1.0, 0.0).astype(F32)

    row8 = iota((8, 128), 0)
    for copy in fetched[:3]:
        copy.wait()
    for x in range(8):
        u, g, wa, wb = noisy[x], -TAU * upstream[x], weights[0, x], weights[1, x]
        send_x[x] = jnp.concatenate([u, g, wa, wb], axis=0).astype(BF16)
        top = jnp.where(row8 < 5, pltpu.roll(u, 5, 0), g)
        low = jnp.where(row8 < 4, pltpu.roll(wa, 4, 0), pltpu.roll(wb, 6, 0))
        send_yl[x] = jnp.concatenate([top, low], axis=0).astype(BF16)
        top = jnp.where(row8 < 5, u, pltpu.roll(g, 5, 0))
        low = jnp.where(row8 < 4, wa, pltpu.roll(wb, 4, 0))
        send_yh[x] = jnp.concatenate([top, low], axis=0).astype(BF16)
    pl.semaphore_wait(barrier, len(peers))

    halo = []
    span = {-1: (0, 13), 0: (0, 5), 1: (3, 0)}
    for n, (dx, dy) in enumerate(sides):
        start, land = span[dx]
        if dy == 0:
            src, dst = send_x.at[pl.ds(start, 5)], got_x.at[0 if dx > 0 else 1]
        else:
            count = 8 if dx == 0 else 5
            src = (send_yl if dy > 0 else send_yh).at[pl.ds(start, count)]
            dst = got_y.at[0 if dy > 0 else 1, pl.ds(land, count)]
        copy = pltpu.make_async_remote_copy(
            src_ref=src, dst_ref=dst, send_sem=halo_send.at[n], recv_sem=halo_recv.at[n],
            device_id=near(dx, dy), device_id_type=MESH,
        )
        copy.start()
        halo.append(copy)

    eye = iota((CH, CH), 0) == iota((CH, CH), 1)
    for copy in fetched[3:]:
        copy.wait()
    pad_in[...] = jnp.zeros_like(pad_in)
    pad_out[...] = jnp.zeros_like(pad_out)
    whole_in, whole_out = filter_in[...].astype(F32), filter_out[...].astype(F32)
    cols = []
    for k in range(2):
        pad_in[k, 0:27, :] = whole_in[:, k, :]
        pad_out[k, 0:27, :] = whole_out[:, k, :]
        spread = jnp.broadcast_to(bias[k : k + 1, :], (CH, CH))
        cols.append(jnp.sum(jnp.where(eye, spread, 0.0), axis=1, keepdims=True))
    win_t = [pad_in[k].astype(BF16) for k in range(2)]
    wout = [pad_out[k].astype(BF16) for k in range(2)]
    win = [dot_nt(one_hot(eye), win_t[k]).astype(BF16) for k in range(2)]
    wout_t = [dot_nt(one_hot(eye), wout[k]).astype(BF16) for k in range(2)]
    for n in range(4):
        picks[n] = pick_columns(n // 2, n % 2 == 1)
    fill_patch(t1a, win[0], cols[0], range(-4, 12))
    fill_gather(toa, wout[0], range(-4, 12), 1, myl, myh)
    fill_patch(t1b, win[1], cols[1], range(-2, 10))
    fill_spread(t2b, wout_t[1], range(-2, 10))
    fill_gather(t3b, win_t[1], range(-2, 10), -1, myl, myh)
    fill_spread(t2a, wout_t[0], range(0, 8))
    fill_gather(t3a, win_t[0], range(0, 8), -1, myl, myh)

    for copy in halo:
        copy.wait()

    for i in range(LAYERS_X):
        if i < XOFF:
            rows, edge = got_x[0, i].astype(F32) * mxl, mxl
        elif i >= XOFF + 8:
            rows, edge = got_x[1, i - XOFF - 8].astype(F32) * mxh, mxh
        else:
            x, edge = i - XOFF, jnp.float32(1.0)
            rows = jnp.concatenate([noisy[x], upstream[x], weights[0, x], weights[1, x]], axis=0)
        lo = got_y[0, i].astype(F32) * (edge * myl)
        hi = got_y[1, i].astype(F32) * (edge * myh)
        lo_t, lo_b, hi_t, hi_b = lo[0:8], lo[8:16], hi[0:8], hi[8:16]
        u = jnp.concatenate([pltpu.roll(lo_t, 3, 0), rows[0:8], hi_t], axis=0)
        u0[i] = u
        su0[i] = slab_of(u)
        w0[i] = jnp.concatenate([pltpu.roll(lo_b, 4, 0), rows[16:24], hi_b], axis=0)
        if 2 <= i < 16:
            own = XOFF <= i < XOFF + 8
            mid = rows[8:16]
            lo_g, hi_g = lo_t, pltpu.roll(hi_t, 3, 0)
            ss1[i] = slab_of(jnp.concatenate([lo_g, -TAU * mid if own else mid, hi_g], axis=0))
            back = -1.0 / TAU
            g0[i] = jnp.concatenate([lo_g * back, mid if own else mid * back, hi_g * back], axis=0)
            w1[i] = jnp.concatenate(
                [pltpu.roll(lo_b, 2, 0), rows[24:32], pltpu.roll(hi_b, 4, 0)], axis=0
            )

    row24 = iota((ROWS, 128), 0)
    inside_y = jnp.where(row24 < 8, myl, jnp.where(row24 < 16, 1.0, myh))

    def x_mask(i):
        return jnp.where(i < XOFF, mxl, jnp.where(i >= XOFF + 8, mxh, 1.0))

    def forward(p, keep):
        slot = jnp.where(p < 6, p - 2, 4)
        i = 1 + 2 * p
        rhs = pair_of(su0, i)
        q = None
        for m in range(4):
            cut = slice(4 * CH * m, 4 * CH * (m + 1))
            half = dot(t1a[cut, :], rhs)
            t = jnp.tanh(half)
            h = half + half * t
            hb = h.astype(BF16)
            if keep and m in (1, 2):
                own = slice(4 * CH * (m - 1), 4 * CH * m)
                h0[slot, own, :] = hb
                d0[slot, own, :] = (1.0 + t) + (h - h * t)
            term = dot(toa[:, cut], hb)
            q = term if q is None else q + term
        qbuf[2 * p] = q[:, 0:128] * x_mask(i)
        qbuf[2 * p + 1] = q[:, 128:256] * x_mask(i + 1)

    def iterate(n):
        i = n + 2
        learned = gather_sum(qbuf, n, 1)
        v = u0[i] - TAU * (smooth_at(u0, w0, i) + learned)
        su1[i] = slab_of(v * (inside_y * x_mask(i)))

    @pl.loop(0, 2, unroll=2)
    def _(p):
        forward(p, False)

    @pl.loop(2, 8, unroll=2)
    def _(p):
        iterate(2 * p - 4)
        iterate(2 * p - 3)
        forward(p, True)

    iterate(12)
    iterate(13)

    def middle(p, slot):
        i = 3 + 2 * p
        rhs_u, rhs_s = pair_of(su1, i), pair_of(ss1, i)
        q = None
        for first, last in ((0, 2), (2, 6), (6, 10), (10, 12)):
            cut = slice(CH * first, CH * last)
            half = dot(t1b[cut, :], rhs_u)
            dh = dot(t2b[cut, :], rhs_s)
            t = jnp.tanh(half)
            h = half + half * t
            dab = (dh * ((1.0 + t) + (h - h * t))).astype(BF16)
            if last - first == 4:
                own = slice(CH * (first - 2), CH * (last - 2))
                h1[slot, own, :] = h.astype(BF16)
                dab1[slot, own, :] = dab
            term = dot(t3b[:, cut], dab)
            q = term if q is None else q + term
        pbuf[2 * p] = q[:, 0:128] * x_mask(i)
        pbuf[2 * p + 1] = q[:, 128:256] * x_mask(i + 1)

    def cotangent(n):
        i = n + 4
        g = g0[i]
        v = g - TAU * (g + smooth_at(g0, w1, i)) + gather_sum(pbuf, n, -1)
        v = v * (inside_y * x_mask(i))
        g1[i] = v
        ss0[i] = slab_of(-TAU * v)

    @pl.loop(0, 2, unroll=2)
    def _(p):
        middle(p, jnp.where(p > 0, 0, 4))

    @pl.loop(2, 6, unroll=2)
    def _(p):
        cotangent(2 * p - 4)
        cotangent(2 * p - 3)
        middle(p, jnp.where(p < 5, p - 1, 4))

    cotangent(8)
    cotangent(9)

    def beside(store):
        return jnp.concatenate([store[p] for p in range(4)], axis=1)

    sums = packed_sums(dot_nt(beside(h1), layers_beside(ss1)), picks[2])
    sums = sums + packed_sums(dot_nt(beside(dab1), layers_beside(su1)), picks[3])

    @pl.loop(0, 4, unroll=4)
    def _(p):
        dh = dot(t2a[...], pair_of(ss0, XOFF + 2 * p))
        dab0[p] = (dh * d0[p]).astype(BF16)

    sums = sums + packed_sums(dot_nt(beside(h0), layers_beside(ss0)), picks[0])
    sums = sums + packed_sums(dot_nt(beside(dab0), layers_beside(su0)), picks[1])
    for n in range(2):
        pack[n] = sums[32 * n : 32 * n + 32]

    first = []
    for s in far_first:
        to, peer = in_group(s)
        copy = pltpu.make_async_remote_copy(
            src_ref=pack.at[lax.rem(to, 2)], dst_ref=red_g.at[me_g],
            send_sem=red_send.at[0, s], recv_sem=red_recv.at[0, s],
            device_id=peer, device_id_type=MESH,
        )
        copy.start()
        first.append(copy)
    red_g[me_g] = pack[core]

    pbuf[0] = jnp.zeros_like(pbuf[0])
    pbuf[1] = jnp.zeros_like(pbuf[1])
    pbuf[10] = jnp.zeros_like(pbuf[0])
    pbuf[11] = jnp.zeros_like(pbuf[0])

    @pl.loop(0, 4, unroll=2)
    def _(p):
        q = dot(t3a[...], dab0[p])
        pbuf[2 * p + 2] = q[:, 0:128]
        pbuf[2 * p + 3] = q[:, 128:256]

    for n in range(10):
        part[n] = gather_sum(pbuf, n, -1)
    ring_x[0] = part[0, 8:16, :]
    ring_x[1] = part[9, 8:16, :]
    for side, row in ((0, 7), (1, 16)):
        ring_y[side] = jnp.concatenate([part[n, row : row + 1, :] for n in range(1, 9)], axis=0)
        for end, n in ((0, 0), (1, 9)):
            ring_c[end, side] = jnp.broadcast_to(part[n, row : row + 1, :], (8, 128))

    around = []
    for n, (dx, dy) in enumerate(sides):
        a, b = (0 if dx < 0 else 1), (0 if dy < 0 else 1)
        if dy == 0:
            src, dst = ring_x.at[a], back_x.at[a]
        elif dx == 0:
            src, dst = ring_y.at[b], back_y.at[b]
        else:
            src, dst = ring_c.at[a, b], back_c.at[a, b]
        copy = pltpu.make_async_remote_copy(
            src_ref=src, dst_ref=dst, send_sem=ring_send.at[n], recv_sem=ring_recv.at[n],
            device_id=near(dx, dy), device_id_type=MESH,
        )
        copy.start()
        around.append(copy)

    for copy in first:
        copy.wait()
    tile_y[...] = sum_slots(red_g)

    second = []
    for s in sorted(range(1, ny), key=lambda s: -min(s, ny - s)):
        copy = pltpu.make_async_remote_copy(
            src_ref=tile_y, dst_ref=red_y.at[py],
            send_sem=red_send.at[1, s], recv_sem=red_recv.at[1, s],
            device_id=along_y(s), device_id_type=MESH,
        )
        copy.start()
        second.append(copy)
    red_y[py] = tile_y[...]

    for copy in around:
        copy.wait()
    for x in range(8):
        i = x + XOFF
        back = part[x + 1, 8:16, :]
        add_lo = back_y[1, x : x + 1, :] * myl
        add_hi = back_y[0, x : x + 1, :] * myh
        if x == 0:
            back = back + back_x[1] * mxl
            add_lo = add_lo + back_c[1, 1, 0:1, :] * (mxl * myl)
            add_hi = add_hi + back_c[1, 0, 0:1, :] * (mxl * myh)
        if x == 7:
            back = back + back_x[0] * mxh
            add_lo = add_lo + back_c[0, 1, 0:1, :] * (mxh * myl)
            add_hi = add_hi + back_c[0, 0, 0:1, :] * (mxh * myh)
        back = back + jnp.where(row8 == 0, add_lo, 0.0) + jnp.where(row8 == 7, add_hi, 0.0)
        smooth = smooth_at(g1, w0, i)[8:16]
        out_grad[x] = g1[i, 8:16, :] - TAU * smooth + back + TAU * upstream[x]

    for copy in second:
        copy.wait()
    tile_z[...] = sum_slots(red_y)
    third = []
    for s in sorted(range(1, nz), key=lambda s: -min(s, nz - s)):
        copy = pltpu.make_async_remote_copy(
            src_ref=tile_z, dst_ref=red_z.at[pz],
            send_sem=red_send.at[2, s], recv_sem=red_recv.at[2, s],
            device_id=along_z(s), device_id_type=MESH,
        )
        copy.start()
        third.append(copy)
    red_z[pz] = tile_z[...]
    for copy in third:
        copy.wait()
    tile_f[...] = sum_slots(red_z)
    other = pltpu.make_async_remote_copy(
        src_ref=tile_f, dst_ref=final.at[core],
        send_sem=red_send.at[3, 0], recv_sem=red_recv.at[3, 0],
        device_id=in_group(jnp.where(core > 0, 7, 1))[1], device_id_type=MESH,
    )
    other.start()
    final[core] = tile_f[...]
    other.wait()

    scale = 1.0 / 2048.0
    whole = final[...].reshape(CH, 128) * scale
    turned = whole.T
    for k in range(2):
        out_p[:, k, 0:64] = turned[64 * k : 64 * k + 28, :]
        out_p[0:27, k, 64:128] = turned[64 * k + 32 : 64 * k + 59, :]


def sum_slots(store):
    total = store[0]
    for n in range(1, store.shape[0]):
        total = total + store[n]
    return total


def body(noisy, weights, filter_in, bias, filter_out, upstream):
    size_x, size_y = lax.axis_size("gx"), lax.axis_size("gy")
    field = pltpu.VMEM((LAYERS_X, ROWS, 128), F32)
    stack = pltpu.VMEM((LAYERS_X, SLAB, 128), BF16)
    vm = lambda *shape: pltpu.VMEM(shape, F32)
    vb = lambda *shape: pltpu.VMEM(shape, BF16)
    dma = lambda *shape: pltpu.SemaphoreType.DMA(shape)
    scratch = [
        vm(8, 8, 128), vm(2, 8, 8, 128), vb(27, 2, CH), vm(2, CH), vb(27, 2, CH), vm(8, 8, 128),
        vb(8, 32, 128), vb(8, 16, 128), vb(8, 16, 128), vb(2, 5, 32, 128), vb(2, LAYERS_X, 16, 128),
        field, field, field, field, field, field,
        stack, stack, stack, stack,
        vb(16 * CH, DEPTH), vb(12 * CH, DEPTH), vb(12 * CH, DEPTH), vb(8 * CH, DEPTH),
        vb(9 * GROWS, 16 * CH), vb(9 * GROWS, 12 * CH), vb(9 * GROWS, 8 * CH),
        vm(2, 32, CH), vm(2, 32, CH), vb(4, 256, 128),
        vm(16, 9 * GROWS, 128), vm(12, 9 * GROWS, 128),
        vb(5, 8 * CH, 256), vm(5, 8 * CH, 256), vb(5, 8 * CH, 256), vb(5, 8 * CH, 256), vb(4, 8 * CH, 256),
        vm(2, 8, 128), vm(2, 8, 128), vm(2, 2, 8, 128), vm(2, 8, 128), vm(2, 8, 128), vm(2, 2, 8, 128), vm(10, ROWS, 128),
        vm(2, 32, 128), vm(8, 32, 128), vm(size_x // 4, 32, 128), vm(size_y // 2, 32, 128),
        vm(32, 128), vm(32, 128), vm(32, 128), vm(2, 32, 128),
        dma(6), dma(8), dma(8), dma(8), dma(8), dma(4, 8), dma(4, 8),
    ]
    spec = pl.BlockSpec(memory_space=pltpu.VMEM)
    far = pl.BlockSpec(memory_space=pltpu.HBM)
    shapes = (vm(8, 8, 128), vm(28, 2, 128))
    grad, sums = pl.pallas_call(
        functools.partial(kernel, size_x, size_y),
        out_shape=shapes,
        in_specs=[far] * 6,
        out_specs=(spec,) * 2,
        scratch_shapes=scratch,
        compiler_params=pltpu.CompilerParams(
            collective_id=0, has_side_effects=True, vmem_limit_bytes=60 * 1024 * 1024
        ),
    )(
        noisy, weights, jnp.transpose(filter_in, (2, 0, 1)), bias,
        jnp.transpose(filter_out, (1, 0, 2)), upstream,
    )
    w1, w2, b = sums[:27, :, :64], sums[:27, :, 64:], sums[27, :, :64]
    return grad, jnp.transpose(w1, (1, 2, 0)), jnp.transpose(w2, (1, 0, 2)), b


def solution(mesh):
    return jax.shard_map(
        body,
        mesh=mesh,
        in_specs=(
            P("gx", "gy", None),
            P(None, "gx", "gy", None),
            P(),
            P(),
            P(),
            P("gx", "gy", None),
        ),
        out_specs=(P("gx", "gy", None), P(), P(), P()),
        check_vma=False,
    )
```

```python
import functools

import jax
import jax.numpy as jnp
from jax import lax
from jax.experimental import pallas as pl
from jax.experimental.pallas import tpu as pltpu
from jax.sharding import PartitionSpec as P

TAU = 0.15
F32 = jnp.float32
BF16 = jnp.bfloat16
MESH = pl.DeviceIdType.MESH
CH = 64
ROWS = 24
XOFF = 5
LAYERS_X = 18
SLAB = 80
DEPTH = 3 * SLAB
GROWS = 16
GBASE = 4


def iota(shape, axis):
    return lax.broadcasted_iota(jnp.int32, shape, axis)


def move_z(v, step):
    lane = iota(v.shape, 1)
    if step == 1:
        return jnp.where(lane == 127, 0.0, pltpu.roll(v, 127, 1))
    return jnp.where(lane == 0, 0.0, pltpu.roll(v, 1, 1))


def move_y(v, step):
    return pltpu.roll(v, (-step) % v.shape[0], 0)


def slab_of(v):
    ones = jnp.ones((SLAB - 3 * ROWS, 128), F32)
    return jnp.concatenate([move_z(v, -1), v, move_z(v, 1), ones], axis=0).astype(BF16)


def flux_x(v, w, i):
    return w[i] * (v[i + 1] - v[i])


def smooth_at(v, w, i):
    here, factor = v[i], w[i]
    fy = factor * (move_y(here, 1) - here)
    fz = factor * (move_z(here, 1) - here)
    return (
        flux_x(v, w, i - 1) - flux_x(v, w, i) + (move_y(fy, -1) - fy) + (move_z(fz, -1) - fz)
    )


def split_column(shape, axis):
    k = iota(shape, axis)
    sx = (k >= SLAB).astype(jnp.int32) + (k >= 2 * SLAB).astype(jnp.int32)
    rest = k - SLAB * sx
    sz = (rest >= ROWS).astype(jnp.int32) + (rest >= 2 * ROWS).astype(jnp.int32)
    row = rest - ROWS * sz
    good = (rest < 3 * ROWS) & (k < DEPTH)
    return sx, sz, row, good, rest


def split_rows(shape, axis):
    m = iota(shape, axis)
    s = sum((m >= GROWS * n).astype(jnp.int32) for n in range(1, 9))
    row = m - GROWS * s + GBASE
    sx = (s >= 3).astype(jnp.int32) + (s >= 6).astype(jnp.int32)
    return sx, s - 3 * sx, row


def one_hot(hit):
    return jnp.where(hit, 1.0, 0.0).astype(BF16)


def dot(a, b):
    return jnp.dot(a, b, preferred_element_type=F32)


def dot_nt(a, b):
    return lax.dot_general(a, b, (((1,), (1,)), ((), ())), preferred_element_type=F32)


def thirds(v):
    high = v.astype(BF16)
    rest = v - high.astype(F32)
    mid = rest.astype(BF16)
    low = (rest - mid.astype(F32)).astype(BF16)
    return high, mid, low


def fill_patch(out, weight, bias_col, ys):
    shape = (32, DEPTH)
    sx, sz, row, good, _ = split_column(shape, 1)
    base = 9 * sx + sz
    j = iota(shape, 0)
    k = iota((CH, DEPTH), 1)
    extra = jnp.zeros((CH, DEPTH), F32)
    for n, part in enumerate(thirds(bias_col)):
        extra = extra + jnp.where(k == SLAB + 3 * ROWS + n, part.astype(F32), 0.0)
    for n, y in enumerate(ys):
        step = row - (y + 7)
        hit = good & (step >= 0) & (step <= 2) & (j == base + 3 * step)
        block = (dot(weight, one_hot(hit)) + extra) * 0.5
        out[n * CH : (n + 1) * CH, :] = block.astype(BF16)


def fill_spread(out, weight_t, ys):
    shape = (32, DEPTH)
    sx, sz, row, good, _ = split_column(shape, 1)
    base = 9 * (2 - sx) + (2 - sz)
    j = iota(shape, 0)
    for n, y in enumerate(ys):
        step = (y + 9) - row
        hit = good & (step >= 0) & (step <= 2) & (j == base + 3 * step)
        out[n * CH : (n + 1) * CH, :] = (dot(weight_t, one_hot(hit)) * 0.5).astype(BF16)


def fill_gather(out, weight, ys, sign, low, high):
    shape = (9 * GROWS, 32)
    sx, sz, row = split_rows(shape, 0)
    base = 9 * sx + sz
    j = iota(shape, 1)
    for n in range(0, len(ys), 2):
        halves = []
        for y in ys[n : n + 2]:
            step = (y + 9) - row if sign > 0 else row - (y + 7)
            hit = (step >= 0) & (step <= 2) & (j == base + 3 * step)
            part = one_hot(hit)
            half = dot(part, weight)
            if y < 0:
                half = half * low
            elif y > 7:
                half = half * high
            halves.append(half)
        out[:, n * CH : (n + 2) * CH] = jnp.concatenate(halves, axis=1).astype(BF16)


def pair_of(stack, i):
    left = stack[pl.ds(i - 1, 3)].reshape(DEPTH, 128)
    right = stack[pl.ds(i, 3)].reshape(DEPTH, 128)
    return jnp.concatenate([left, right], axis=1)


def gather_sum(store, n, sign):
    total = None
    for sz in range(3):
        part = None
        for sx in range(3):
            at = n + sx if sign > 0 else n + 2 - sx
            lo = (3 * sx + sz) * GROWS
            term = store[at, lo : lo + GROWS, :]
            part = term if part is None else part + term
        if sz != 1:
            part = move_z(part, sign * (sz - 1))
        total = part if total is None else total + part
    pad = jnp.zeros((GBASE, 128), F32)
    return jnp.concatenate([pad, total, pad], axis=0)


def fold_rows(out):
    total = out[0:CH]
    for y in range(1, 8):
        total = total + pltpu.roll(out[y * CH : (y + 1) * CH], 256 - y, 1)
    return total


def pick_columns(layer, first):
    shape = (256, 128)
    sx, sz, row, good, rest = split_column(shape, 0)
    lane = iota(shape, 1)
    if first:
        step = row - 7
        j = 9 * sx + 3 * step + sz
        ok = good & (step >= 0) & (step <= 2)
        hit = ok & (lane == 64 * layer + j)
        spare = (sx == 1) & (rest == 3 * ROWS) & (lane == 64 * layer + 27)
        return one_hot(hit | spare)
    step = 9 - row
    j = 9 * (2 - sx) + 3 * step + (2 - sz)
    ok = good & (step >= 0) & (step <= 2)
    return one_hot(ok & (lane == 64 * layer + 32 + j))


def packed_sums(out, pick):
    folded = fold_rows(out)
    high, mid, low = thirds(folded)
    return dot(high, pick) + dot(mid, pick) + dot(low, pick)


def layers_beside(stack):
    parts = [stack[i - 1 : i + 2].reshape(DEPTH, 128) for i in range(XOFF, XOFF + 8)]
    whole = jnp.concatenate(parts, axis=1)
    return jnp.concatenate([whole, jnp.zeros((256 - DEPTH, 1024), BF16)], axis=0)


def kernel(
    size_x, size_y,
    noisy_at, weights_at, filter_in_at, bias_at, filter_out_at, upstream_at,
    out_grad, out_p,
    noisy, weights, filter_in, bias, filter_out, upstream,
    send_x, send_yl, send_yh, got_x, got_y,
    u0, g0, w0, w1, u1, g1,
    su0, ss1, su1, ss0,
    t1a, t1b, t2b, t2a, toa, t3b, t3a,
    pad_in, pad_out, picks,
    qbuf, pbuf, h0, d0, h1, dab1, dab0,
    ring_x, ring_y, ring_c, back_x, back_y, back_c, part,
    pack, red_g, red_y, red_z, tile_y, tile_z, tile_f, final,
    fetch_sem, halo_send, halo_recv, ring_send, ring_recv, red_send, red_recv,
):
    gx, gy = lax.axis_index("gx"), lax.axis_index("gy")
    core, xlo, py = lax.rem(gx, 2), lax.rem(gx // 2, 2), gx // 4
    xhi, pz = lax.rem(gy, 2), gy // 2
    ny, nz = size_x // 4, size_y // 2
    me_g = (xhi * 2 + xlo) * 2 + core

    def near(dx, dy):
        return (lax.rem(gx + dx + size_x, size_x), lax.rem(gy + dy + size_y, size_y))

    def in_group(step):
        to = lax.rem(me_g + step, 8)
        c, x = lax.rem(to, 2), to // 2
        return to, (py * 4 + lax.rem(x, 2) * 2 + c, pz * 2 + x // 2)

    def along_y(step):
        return (lax.rem(py + step, ny) * 4 + xlo * 2 + core, gy)

    def along_z(step):
        return (gx, lax.rem(pz + step, nz) * 2 + xhi)

    sides = [(-1, -1), (1, 1), (-1, 1), (1, -1), (0, -1), (0, 1), (-1, 0), (1, 0)]
    far_first = (4, 3, 5, 2, 6, 1, 7)
    barrier = pltpu.get_barrier_semaphore()
    peers = [near(*side) for side in sides] + [in_group(s)[1] for s in range(1, 8)]
    peers += [along_y(s) for s in range(1, ny)] + [along_z(s) for s in range(1, nz)]
    for peer in peers[: len(sides)]:
        pl.semaphore_signal(barrier, inc=1, device_id=peer, device_id_type=MESH)
    fetched = [
        pltpu.make_async_copy(src, dst, fetch_sem.at[n])
        for n, (src, dst) in enumerate((
            (noisy_at, noisy), (upstream_at, upstream), (weights_at, weights),
            (filter_in_at, filter_in), (filter_out_at, filter_out), (bias_at, bias),
        ))
    ]
    for copy in fetched:
        copy.start()
    for peer in peers[len(sides) :]:
        pl.semaphore_signal(barrier, inc=1, device_id=peer, device_id_type=MESH)

    mxl = jnp.where(gx > 0, 1.0, 0.0).astype(F32)
    mxh = jnp.where(gx < size_x - 1, 1.0, 0.0).astype(F32)
    myl = jnp.where(gy > 0, 1.0, 0.0).astype(F32)
    myh = jnp.where(gy < size_y - 1, 1.0, 0.0).astype(F32)

    row8 = iota((8, 128), 0)
    for copy in fetched[:3]:
        copy.wait()
    for x in range(8):
        u, g, wa, wb = noisy[x], -TAU * upstream[x], weights[0, x], weights[1, x]
        send_x[x] = jnp.concatenate([u, g, wa, wb], axis=0).astype(BF16)
        top = jnp.where(row8 < 5, pltpu.roll(u, 5, 0), g)
        low = jnp.where(row8 < 4, pltpu.roll(wa, 4, 0), pltpu.roll(wb, 6, 0))
        send_yl[x] = jnp.concatenate([top, low], axis=0).astype(BF16)
        top = jnp.where(row8 < 5, u, pltpu.roll(g, 5, 0))
        low = jnp.where(row8 < 4, wa, pltpu.roll(wb, 4, 0))
        send_yh[x] = jnp.concatenate([top, low], axis=0).astype(BF16)
    pl.semaphore_wait(barrier, len(peers))

    halo = []
    span = {-1: (0, 13), 0: (0, 5), 1: (3, 0)}
    for n, (dx, dy) in enumerate(sides):
        start, land = span[dx]
        if dy == 0:
            src, dst = send_x.at[pl.ds(start, 5)], got_x.at[0 if dx > 0 else 1]
        else:
            count = 8 if dx == 0 else 5
            src = (send_yl if dy > 0 else send_yh).at[pl.ds(start, count)]
            dst = got_y.at[0 if dy > 0 else 1, pl.ds(land, count)]
        copy = pltpu.make_async_remote_copy(
            src_ref=src, dst_ref=dst, send_sem=halo_send.at[n], recv_sem=halo_recv.at[n],
            device_id=near(dx, dy), device_id_type=MESH,
        )
        copy.start()
        halo.append(copy)

    eye = iota((CH, CH), 0) == iota((CH, CH), 1)
    for copy in fetched[3:]:
        copy.wait()
    pad_in[...] = jnp.zeros_like(pad_in)
    pad_out[...] = jnp.zeros_like(pad_out)
    whole_in, whole_out = filter_in[...].astype(F32), filter_out[...].astype(F32)
    cols = []
    for k in range(2):
        pad_in[k, 0:27, :] = whole_in[:, k, :]
        pad_out[k, 0:27, :] = whole_out[:, k, :]
        spread = jnp.broadcast_to(bias[k : k + 1, :], (CH, CH))
        cols.append(jnp.sum(jnp.where(eye, spread, 0.0), axis=1, keepdims=True))
    win_t = [pad_in[k].astype(BF16) for k in range(2)]
    wout = [pad_out[k].astype(BF16) for k in range(2)]
    win = [dot_nt(one_hot(eye), win_t[k]).astype(BF16) for k in range(2)]
    wout_t = [dot_nt(one_hot(eye), wout[k]).astype(BF16) for k in range(2)]
    for n in range(4):
        picks[n] = pick_columns(n // 2, n % 2 == 1)
    fill_patch(t1a, win[0], cols[0], range(-4, 12))
    fill_gather(toa, wout[0], range(-4, 12), 1, myl, myh)
    fill_patch(t1b, win[1], cols[1], range(-2, 10))
    fill_spread(t2b, wout_t[1], range(-2, 10))
    fill_gather(t3b, win_t[1], range(-2, 10), -1, myl, myh)
    fill_spread(t2a, wout_t[0], range(0, 8))
    fill_gather(t3a, win_t[0], range(0, 8), -1, myl, myh)

    for copy in halo:
        copy.wait()

    for i in range(LAYERS_X):
        if i < XOFF:
            rows, edge = got_x[0, i].astype(F32) * mxl, mxl
        elif i >= XOFF + 8:
            rows, edge = got_x[1, i - XOFF - 8].astype(F32) * mxh, mxh
        else:
            x, edge = i - XOFF, jnp.float32(1.0)
            rows = jnp.concatenate([noisy[x], upstream[x], weights[0, x], weights[1, x]], axis=0)
        lo = got_y[0, i].astype(F32) * (edge * myl)
        hi = got_y[1, i].astype(F32) * (edge * myh)
        lo_t, lo_b, hi_t, hi_b = lo[0:8], lo[8:16], hi[0:8], hi[8:16]
        u = jnp.concatenate([pltpu.roll(lo_t, 3, 0), rows[0:8], hi_t], axis=0)
        u0[i] = u
        su0[i] = slab_of(u)
        w0[i] = jnp.concatenate([pltpu.roll(lo_b, 4, 0), rows[16:24], hi_b], axis=0)
        if 2 <= i < 16:
            own = XOFF <= i < XOFF + 8
            mid = rows[8:16]
            lo_g, hi_g = lo_t, pltpu.roll(hi_t, 3, 0)
            ss1[i] = slab_of(jnp.concatenate([lo_g, -TAU * mid if own else mid, hi_g], axis=0))
            back = -1.0 / TAU
            g0[i] = jnp.concatenate([lo_g * back, mid if own else mid * back, hi_g * back], axis=0)
            w1[i] = jnp.concatenate(
                [pltpu.roll(lo_b, 2, 0), rows[24:32], pltpu.roll(hi_b, 4, 0)], axis=0
            )

    row24 = iota((ROWS, 128), 0)
    inside_y = jnp.where(row24 < 8, myl, jnp.where(row24 < 16, 1.0, myh))

    def x_mask(i):
        return jnp.where(i < XOFF, mxl, jnp.where(i >= XOFF + 8, mxh, 1.0))

    def forward(p, keep):
        slot = jnp.where(p < 6, p - 2, 4)
        i = 1 + 2 * p
        rhs = pair_of(su0, i)
        q = None
        for m in range(4):
            cut = slice(4 * CH * m, 4 * CH * (m + 1))
            half = dot(t1a[cut, :], rhs)
            t = jnp.tanh(half)
            h = half + half * t
            hb = h.astype(BF16)
            if keep and m in (1, 2):
                own = slice(4 * CH * (m - 1), 4 * CH * m)
                h0[slot, own, :] = hb
                d0[slot, own, :] = (1.0 + t) + (h - h * t)
            term = dot(toa[:, cut], hb)
            q = term if q is None else q + term
        qbuf[2 * p] = q[:, 0:128] * x_mask(i)
        qbuf[2 * p + 1] = q[:, 128:256] * x_mask(i + 1)

    def iterate(n):
        i = n + 2
        learned = gather_sum(qbuf, n, 1)
        v = u0[i] - TAU * (smooth_at(u0, w0, i) + learned)
        su1[i] = slab_of(v * (inside_y * x_mask(i)))

    @pl.loop(0, 2, unroll=2)
    def _(p):
        forward(p, False)

    @pl.loop(2, 8, unroll=3)
    def _(p):
        iterate(2 * p - 4)
        iterate(2 * p - 3)
        forward(p, True)

    iterate(12)
    iterate(13)

    def middle(p, slot):
        i = 3 + 2 * p
        rhs_u, rhs_s = pair_of(su1, i), pair_of(ss1, i)
        q = None
        for first, last in ((0, 2), (2, 6), (6, 10), (10, 12)):
            cut = slice(CH * first, CH * last)
            half = dot(t1b[cut, :], rhs_u)
            dh = dot(t2b[cut, :], rhs_s)
            t = jnp.tanh(half)
            h = half + half * t
            dab = (dh * ((1.0 + t) + (h - h * t))).astype(BF16)
            if last - first == 4:
                own = slice(CH * (first - 2), CH * (last - 2))
                h1[slot, own, :] = h.astype(BF16)
                dab1[slot, own, :] = dab
            term = dot(t3b[:, cut], dab)
            q = term if q is None else q + term
        pbuf[2 * p] = q[:, 0:128] * x_mask(i)
        pbuf[2 * p + 1] = q[:, 128:256] * x_mask(i + 1)

    def cotangent(n):
        i = n + 4
        g = g0[i]
        v = g - TAU * (g + smooth_at(g0, w1, i)) + gather_sum(pbuf, n, -1)
        v = v * (inside_y * x_mask(i))
        g1[i] = v
        ss0[i] = slab_of(-TAU * v)

    @pl.loop(0, 2, unroll=2)
    def _(p):
        middle(p, jnp.where(p > 0, 0, 4))

    @pl.loop(2, 6, unroll=4)
    def _(p):
        cotangent(2 * p - 4)
        cotangent(2 * p - 3)
        middle(p, jnp.where(p < 5, p - 1, 4))

    cotangent(8)
    cotangent(9)

    def beside(store):
        return jnp.concatenate([store[p] for p in range(4)], axis=1)

    sums = packed_sums(dot_nt(beside(h1), layers_beside(ss1)), picks[2])
    sums = sums + packed_sums(dot_nt(beside(dab1), layers_beside(su1)), picks[3])

    @pl.loop(0, 4, unroll=4)
    def _(p):
        dh = dot(t2a[...], pair_of(ss0, XOFF + 2 * p))
        dab0[p] = (dh * d0[p]).astype(BF16)

    sums = sums + packed_sums(dot_nt(beside(h0), layers_beside(ss0)), picks[0])
    sums = sums + packed_sums(dot_nt(beside(dab0), layers_beside(su0)), picks[1])
    for n in range(2):
        pack[n] = sums[32 * n : 32 * n + 32]

    first = []
    for s in far_first:
        to, peer = in_group(s)
        copy = pltpu.make_async_remote_copy(
            src_ref=pack.at[lax.rem(to, 2)], dst_ref=red_g.at[me_g],
            send_sem=red_send.at[0, s], recv_sem=red_recv.at[0, s],
            device_id=peer, device_id_type=MESH,
        )
        copy.start()
        first.append(copy)
    red_g[me_g] = pack[core]

    pbuf[0] = jnp.zeros_like(pbuf[0])
    pbuf[1] = jnp.zeros_like(pbuf[1])
    pbuf[10] = jnp.zeros_like(pbuf[0])
    pbuf[11] = jnp.zeros_like(pbuf[0])

    @pl.loop(0, 4, unroll=2)
    def _(p):
        q = dot(t3a[...], dab0[p])
        pbuf[2 * p + 2] = q[:, 0:128]
        pbuf[2 * p + 3] = q[:, 128:256]

    for n in range(10):
        part[n] = gather_sum(pbuf, n, -1)
    ring_x[0] = part[0, 8:16, :]
    ring_x[1] = part[9, 8:16, :]
    for side, row in ((0, 7), (1, 16)):
        ring_y[side] = jnp.concatenate([part[n, row : row + 1, :] for n in range(1, 9)], axis=0)
        for end, n in ((0, 0), (1, 9)):
            ring_c[end, side] = jnp.broadcast_to(part[n, row : row + 1, :], (8, 128))

    around = []
    for n, (dx, dy) in enumerate(sides):
        a, b = (0 if dx < 0 else 1), (0 if dy < 0 else 1)
        if dy == 0:
            src, dst = ring_x.at[a], back_x.at[a]
        elif dx == 0:
            src, dst = ring_y.at[b], back_y.at[b]
        else:
            src, dst = ring_c.at[a, b], back_c.at[a, b]
        copy = pltpu.make_async_remote_copy(
            src_ref=src, dst_ref=dst, send_sem=ring_send.at[n], recv_sem=ring_recv.at[n],
            device_id=near(dx, dy), device_id_type=MESH,
        )
        copy.start()
        around.append(copy)

    for copy in first:
        copy.wait()
    tile_y[...] = sum_slots(red_g)

    second = []
    for s in sorted(range(1, ny), key=lambda s: -min(s, ny - s)):
        copy = pltpu.make_async_remote_copy(
            src_ref=tile_y, dst_ref=red_y.at[py],
            send_sem=red_send.at[1, s], recv_sem=red_recv.at[1, s],
            device_id=along_y(s), device_id_type=MESH,
        )
        copy.start()
        second.append(copy)
    red_y[py] = tile_y[...]

    for copy in around:
        copy.wait()
    for x in range(8):
        i = x + XOFF
        back = part[x + 1, 8:16, :]
        add_lo = back_y[1, x : x + 1, :] * myl
        add_hi = back_y[0, x : x + 1, :] * myh
        if x == 0:
            back = back + back_x[1] * mxl
            add_lo = add_lo + back_c[1, 1, 0:1, :] * (mxl * myl)
            add_hi = add_hi + back_c[1, 0, 0:1, :] * (mxl * myh)
        if x == 7:
            back = back + back_x[0] * mxh
            add_lo = add_lo + back_c[0, 1, 0:1, :] * (mxh * myl)
            add_hi = add_hi + back_c[0, 0, 0:1, :] * (mxh * myh)
        back = back + jnp.where(row8 == 0, add_lo, 0.0) + jnp.where(row8 == 7, add_hi, 0.0)
        smooth = smooth_at(g1, w0, i)[8:16]
        out_grad[x] = g1[i, 8:16, :] - TAU * smooth + back + TAU * upstream[x]

    for copy in second:
        copy.wait()
    tile_z[...] = sum_slots(red_y)
    third = []
    for s in sorted(range(1, nz), key=lambda s: -min(s, nz - s)):
        copy = pltpu.make_async_remote_copy(
            src_ref=tile_z, dst_ref=red_z.at[pz],
            send_sem=red_send.at[2, s], recv_sem=red_recv.at[2, s],
            device_id=along_z(s), device_id_type=MESH,
        )
        copy.start()
        third.append(copy)
    red_z[pz] = tile_z[...]
    for copy in third:
        copy.wait()
    tile_f[...] = sum_slots(red_z)
    other = pltpu.make_async_remote_copy(
        src_ref=tile_f, dst_ref=final.at[core],
        send_sem=red_send.at[3, 0], recv_sem=red_recv.at[3, 0],
        device_id=in_group(jnp.where(core > 0, 7, 1))[1], device_id_type=MESH,
    )
    other.start()
    final[core] = tile_f[...]
    other.wait()

    scale = 1.0 / 2048.0
    whole = final[...].reshape(CH, 128) * scale
    turned = whole.T
    for k in range(2):
        out_p[:, k, 0:64] = turned[64 * k : 64 * k + 28, :]
        out_p[0:27, k, 64:128] = turned[64 * k + 32 : 64 * k + 59, :]


def sum_slots(store):
    total = store[0]
    for n in range(1, store.shape[0]):
        total = total + store[n]
    return total


def body(noisy, weights, filter_in, bias, filter_out, upstream):
    size_x, size_y = lax.axis_size("gx"), lax.axis_size("gy")
    field = pltpu.VMEM((LAYERS_X, ROWS, 128), F32)
    stack = pltpu.VMEM((LAYERS_X, SLAB, 128), BF16)
    vm = lambda *shape: pltpu.VMEM(shape, F32)
    vb = lambda *shape: pltpu.VMEM(shape, BF16)
    dma = lambda *shape: pltpu.SemaphoreType.DMA(shape)
    scratch = [
        vm(8, 8, 128), vm(2, 8, 8, 128), vb(27, 2, CH), vm(2, CH), vb(27, 2, CH), vm(8, 8, 128),
        vb(8, 32, 128), vb(8, 16, 128), vb(8, 16, 128), vb(2, 5, 32, 128), vb(2, LAYERS_X, 16, 128),
        field, field, field, field, field, field,
        stack, stack, stack, stack,
        vb(16 * CH, DEPTH), vb(12 * CH, DEPTH), vb(12 * CH, DEPTH), vb(8 * CH, DEPTH),
        vb(9 * GROWS, 16 * CH), vb(9 * GROWS, 12 * CH), vb(9 * GROWS, 8 * CH),
        vm(2, 32, CH), vm(2, 32, CH), vb(4, 256, 128),
        vm(16, 9 * GROWS, 128), vm(12, 9 * GROWS, 128),
        vb(5, 8 * CH, 256), vm(5, 8 * CH, 256), vb(5, 8 * CH, 256), vb(5, 8 * CH, 256), vb(4, 8 * CH, 256),
        vm(2, 8, 128), vm(2, 8, 128), vm(2, 2, 8, 128), vm(2, 8, 128), vm(2, 8, 128), vm(2, 2, 8, 128), vm(10, ROWS, 128),
        vm(2, 32, 128), vm(8, 32, 128), vm(size_x // 4, 32, 128), vm(size_y // 2, 32, 128),
        vm(32, 128), vm(32, 128), vm(32, 128), vm(2, 32, 128),
        dma(6), dma(8), dma(8), dma(8), dma(8), dma(4, 8), dma(4, 8),
    ]
    spec = pl.BlockSpec(memory_space=pltpu.VMEM)
    far = pl.BlockSpec(memory_space=pltpu.HBM)
    shapes = (vm(8, 8, 128), vm(28, 2, 128))
    grad, sums = pl.pallas_call(
        functools.partial(kernel, size_x, size_y),
        out_shape=shapes,
        in_specs=[far] * 6,
        out_specs=(spec,) * 2,
        scratch_shapes=scratch,
        compiler_params=pltpu.CompilerParams(
            collective_id=0, has_side_effects=True, vmem_limit_bytes=60 * 1024 * 1024
        ),
    )(
        noisy, weights, jnp.transpose(filter_in, (2, 0, 1)), bias,
        jnp.transpose(filter_out, (1, 0, 2)), upstream,
    )
    w1, w2, b = sums[:27, :, :64], sums[:27, :, 64:], sums[27, :, :64]
    return grad, jnp.transpose(w1, (1, 2, 0)), jnp.transpose(w2, (1, 0, 2)), b


def solution(mesh):
    return jax.shard_map(
        body,
        mesh=mesh,
        in_specs=(
            P("gx", "gy", None),
            P(None, "gx", "gy", None),
            P(),
            P(),
            P(),
            P("gx", "gy", None),
        ),
        out_specs=(P("gx", "gy", None), P(), P(), P()),
        check_vma=False,
    )
```
